32 devices in a mesh: row: 4 (over y, x), col: 8 (over z, core).
Axes of the slice: x: 2, y: 2, z: 4, core: 2. Of those that a mesh axis runs over, the one named last changes fastest.
Arguments:
- density: bfloat16 [8, 64, 16384], P('row', None, 'col'), may hold values from -0.8984375 to 0.8984375
- density_rows: int32 [8, 8, 32], replicated, may hold values from 0 to 48, as said below
- square_rows: int32 [8, 8, 32], replicated, may hold values from 0 to 48, as said below
- panel_shift: int32 [8], replicated, may hold values from 0 to 48
Outputs:
- purified: float32 [8, 64, 16384], P('row', None, 'col')
The draws below stay inside these ranges and needn't reach their ends.
Inputs may be any that keep to these rules, and one draw needn't show every extreme that they name: `density_rows`: for every tile, 32 distinct block rows in increasing order. `square_rows`: for every tile, 32 distinct block rows in increasing order.
All inputs are finite; a program needn't handle non-finite values.
Results may differ from the reference program's by a relative error of at most 0.0029.
Values may be sent and summed in bfloat16 or wider, within the bound.
No kernel may reach another device: no remote copies, remote signals or barrier semaphores. Data moves between devices by JAX's collectives and lax.ppermute only.
A program may use at most 64 MiB of HBM per device.

```python
import jax
import jax.numpy as jnp
from jax import lax

BLOCK = 64
PANEL = 49
RH = 32
NPAN = 8
N_COL = 8


def draw_rows_common(key):
    scores = jax.random.randint(key, (N_COL, N_COL, PANEL), 0, 1048576) * PANEL
    scores = scores + jnp.arange(PANEL, dtype=jnp.int32)[None, None, :]
    order = jnp.argsort(scores, axis=-1, stable=True).astype(jnp.int32)
    return jnp.sort(order[:, :, :RH], axis=-1).astype(jnp.int32)


def draw_density_rows(key, part):
    return draw_rows_common(jax.random.fold_in(key, 11))


def draw_square_rows(key, part):
    return draw_rows_common(jax.random.fold_in(key, 23))


def set_ends(drawn, stream_key, least, largest):
    dims = drawn.shape
    place = [jax.random.randint(jax.random.fold_in(stream_key, axis), (), 0, dims[axis]) for axis in range(len(dims))]
    drawn = drawn.at[tuple(place)].set(least)
    longest = dims.index(max(dims))
    place[longest] = (place[longest] + 1) % dims[longest]
    return drawn.at[tuple(place)].set(largest)


def block_levels(key, dims, split, low, largest):
    gain = 1.0
    for axis_at, parts in split:
        heights = jax.random.uniform(jax.random.fold_in(jax.random.fold_in(key, 6), axis_at), (parts,), jnp.float32, low / len(split), largest / len(split))
        gain = gain * jnp.repeat(jnp.exp(heights), dims[axis_at] // parts).reshape((-1,) + (1,) * (len(dims) - 1 - axis_at))
    return gain


def noise(own_key, extent, deviation, limit, shards=(), kind=jnp.bfloat16):
    entries = deviation * jax.random.normal(own_key, extent, jnp.float32)
    if shards:
        entries = entries * block_levels(own_key, extent, shards, -0.22, 0.18)
    return jnp.clip(entries, -limit, limit).astype(kind)


def setup_inputs(seed: int = 0) -> dict:
    arg_keys = jax.random.split(jax.random.key(seed), 5)
    density = noise(arg_keys[0], (NPAN, BLOCK, NPAN * RH * BLOCK), 0.15, 0.8984375, ((0, 4), (2, 8)))
    density_rows = draw_density_rows(jax.random.fold_in(arg_keys[4], 71), 0)
    square_rows = draw_square_rows(jax.random.fold_in(arg_keys[4], 71), 0)
    panel_shift = set_ends(jax.random.randint(arg_keys[3], (NPAN,), 0, PANEL), jax.random.fold_in(arg_keys[3], 1), 0, PANEL - 1).astype(jnp.int32)
    return dict(density=density, density_rows=density_rows, square_rows=square_rows, panel_shift=panel_shift)


def tile_product(left_vals, left_rows, right_vals, right_rows, out_rows, panel_shift):
    npan = left_rows.shape[0]
    blk = left_vals.shape[1]
    rh = left_rows.shape[2]
    left_t = jnp.transpose(left_vals.reshape(npan, blk, npan, rh, blk), (0, 2, 3, 1, 4))
    right_t = jnp.transpose(right_vals.reshape(npan, blk, npan, rh, blk), (0, 2, 3, 1, 4))
    slots = jnp.arange(rh, dtype=jnp.int32)
    panels = jnp.arange(npan, dtype=jnp.int32)
    right_rows_t = jnp.transpose(right_rows, (1, 0, 2))

    def one_panel(p):
        crow = out_rows[p]
        arow = left_rows[p]
        match_a = arow[None, None, :, :] == crow[:, :, None, None]
        has_a = jnp.any(match_a, axis=-1)
        a_index = jnp.sum(jnp.where(match_a, slots, 0), axis=-1).astype(jnp.int32)
        target = jnp.mod(crow[:, :, None] + panel_shift[None, None, :] - panel_shift[p], PANEL).astype(jnp.int32)
        match_b = right_rows_t[:, None, :, :] == target[:, :, :, None]
        has_b = jnp.any(match_b, axis=-1)
        b_index = jnp.sum(jnp.where(match_b, slots, 0), axis=-1).astype(jnp.int32)
        a_blocks = left_t[p][panels[None, None, :], a_index].astype(jnp.float32)
        b_blocks = right_t[panels[None, None, :], panels[:, None, None], b_index].astype(jnp.float32)
        weight = jnp.logical_and(has_a, has_b).astype(jnp.float32)
        a_blocks = a_blocks * weight[:, :, :, None, None]
        return jnp.einsum('qekxy,qekyz->qexz', a_blocks, b_blocks)

    result = lax.map(one_panel, panels)
    return jnp.transpose(result, (0, 3, 1, 2, 4)).reshape(npan, blk, npan * rh * blk)


def reference(density, density_rows, square_rows, panel_shift):
    square = tile_product(density, density_rows, density, density_rows, square_rows, panel_shift).astype(jnp.bfloat16)
    cube = tile_product(square, square_rows, density, density_rows, square_rows, panel_shift)
    return 3.0 * square.astype(jnp.float32) - 2.0 * cube
```

```python
import functools

import jax
import jax.numpy as jnp
from jax import lax
from jax.experimental import pallas as pl
from jax.experimental.pallas import tpu as pltpu
from jax.sharding import PartitionSpec as P

PANEL = 49
PIECES = 4

SMEM = pl.BlockSpec(memory_space=pltpu.SMEM)
VMEM = pl.BlockSpec(memory_space=pltpu.VMEM)
HBM = pl.BlockSpec(memory_space=pltpu.HBM)
PARAMS = pltpu.CompilerParams(vmem_limit_bytes=40 * 1024 * 1024)


class Plan:
    def __init__(self, n_row, n_col, blk):
        self.n_row, self.n_col, self.blk = n_row, n_col, blk
        self.ndev = n_row * n_col
        chips = self.ndev // 2
        self.full = min(self.ndev, PANEL)
        self.shared = min(chips, PANEL - self.full)
        self.extra = PANEL - self.full - self.shared
        self.half = blk // 2
        self.piece = blk // PIECES
        self.back_rows = blk + (self.half if self.shared else 0)
        self.rows = self.back_rows + self.piece * self.extra

    def starts(self, u, rows):
        first = u * rows
        step = self.half
        if self.shared:
            chip = u - self.full
            is_full, is_shared = u < self.full, u < self.full + self.shared
            tail = self.ndev * rows + (chip - self.shared) * self.blk
            first = jnp.where(is_full, first, jnp.where(is_shared, 2 * chip * rows + self.blk, tail))
            step = jnp.where(jnp.logical_and(is_shared, jnp.logical_not(is_full)), rows, self.half)
        return [pl.multiple_of(first + h * step, self.piece) for h in range(2)]


def residue(row, shift):
    u = row - shift
    return jnp.where(u < 0, u + PANEL, u)


def kept_lanes(rows, u, shift, blk):
    npan = rows.shape[0]
    target = u + shift
    target = jnp.where(target >= PANEL, target - PANEL, target)
    has = jnp.sum((rows == target).astype(jnp.float32), axis=1, keepdims=True)
    lane = lax.broadcasted_iota(jnp.int32, (npan, npan * blk), 1)
    tile = lax.broadcasted_iota(jnp.int32, (npan, npan * blk), 0)
    return jnp.sum(jnp.where(lane // blk == tile, has, 0.0), axis=0, keepdims=True)


def pack_kernel(plan, x_hbm, rows_hbm, kept_hbm, shift_hbm, out_ref, keep_ref, x_ref, rows_ref, kept_ref, shift_ref, stage, sems):
    row_id, col_id = lax.axis_index("row"), lax.axis_index("col")
    blk, half, piece, ndev = plan.blk, plan.half, plan.piece, plan.ndev
    npan = 2 * plan.n_row
    own = pl.ds(2 * row_id, 2)
    copies = [
        pltpu.make_async_copy(shift_hbm, shift_ref, sems.at[0]),
        pltpu.make_async_copy(rows_hbm.at[own], rows_ref, sems.at[1]),
        pltpu.make_async_copy(x_hbm, x_ref, sems.at[2]),
        pltpu.make_async_copy(kept_hbm, kept_ref, sems.at[3]),
    ]
    for copy in copies:
        copy.start()
    stage[...] = jnp.zeros_like(stage)
    for copy in copies:
        copy.wait()
    for p in range(2):
        shift = shift_ref[2 * row_id + p]
        lanes = slice(p * blk, (p + 1) * blk)
        for e in range(rows_ref.shape[2]):
            u = residue(rows_ref[p, col_id, e], shift)
            block = x_ref[p, :, e * blk : (e + 1) * blk]
            for h, start in enumerate(plan.starts(u, plan.rows)):
                stage[pl.ds(start, half), lanes] = block[h * half : (h + 1) * half]
    for d in range(ndev):
        at = slice(d * plan.rows, d * plan.rows + plan.back_rows)
        out_ref[d, : plan.back_rows] = stage[at]
        group = 2 * (d // plan.n_col % 2) + d % 2
        for k in range(plan.extra):
            start = ndev * plan.rows + k * blk + group * piece
            to = plan.back_rows + k * piece
            out_ref[d, to : to + piece] = stage[start : start + piece]
    me = row_id * plan.n_col + col_id
    sets = [jnp.minimum(me, plan.full - 1), plan.full + me // 2]
    for k, u in enumerate(sets[: keep_ref.shape[0]]):
        for panel in range(npan):
            keep_ref[k, panel : panel + 1] = kept_lanes(kept_ref[panel], u, shift_ref[panel], blk)


def split_pair(low, high):
    blk = low.shape[1] // 2
    first = jnp.concatenate([low[:, :blk], high[:, :blk]], axis=1)
    second = jnp.concatenate([low[:, blk:], high[:, blk:]], axis=1)
    return first, second


def dot(a, b):
    return jnp.dot(a, b, preferred_element_type=jnp.float32)


def purify(s, m):
    return 3.0 * s.astype(jnp.float32) - 2.0 * dot(s, m)


def full_kernel(plan, keep_ref, y_ref, out_ref, m_ref, s_ref):
    blk, n_col = plan.blk, plan.n_col
    for r in range(plan.n_row):
        for j in range(n_col // 2):
            src = r * n_col + 2 * j
            first, second = split_pair(y_ref[src, :blk], y_ref[src + 1, :blk])
            lanes = slice(2 * j * blk, (2 * j + 2) * blk)
            m_ref[2 * r * blk : (2 * r + 1) * blk, lanes] = first
            m_ref[(2 * r + 1) * blk : (2 * r + 2) * blk, lanes] = second
    m = m_ref[...]
    for panel in range(2 * plan.n_row):
        at = slice(panel * blk, (panel + 1) * blk)
        s = dot(m_ref[at], m)
        s_ref[at] = jnp.where(keep_ref[0, panel : panel + 1] > 0, s, 0.0).astype(jnp.bfloat16)
    for r in range(plan.n_row):
        res = purify(s_ref[2 * r * blk : (2 * r + 2) * blk], m).astype(jnp.bfloat16)
        for j in range(n_col // 2):
            lanes = slice(2 * j * blk, (2 * j + 2) * blk)
            first, second = split_pair(res[:blk, lanes], res[blk:, lanes])
            out_ref[r * n_col + 2 * j, :blk] = first
            out_ref[r * n_col + 2 * j + 1, :blk] = second


def shared_kernel(plan, keep_ref, own_ref, far_ref, part_ref, out_ref, *refs):
    *extra_refs, m_ref, s_ref, o_ref = refs
    blk, half, piece, n_col = plan.blk, plan.half, plan.piece, plan.n_col
    first_core = lax.axis_index("col") % 2 == 0
    out_ref[:, :blk] = part_ref[:, :blk]
    for r in range(plan.n_row):
        for j in range(n_col // 2):
            src = r * n_col + 2 * j
            lanes = slice(2 * j * blk, (2 * j + 2) * blk)
            own = split_pair(own_ref[src, :half], own_ref[src + 1, :half])
            far = split_pair(far_ref[src, :half], far_ref[src + 1, :half])
            for p in range(2):
                at = (2 * r + p) * blk
                m_ref[at : at + half, lanes] = jnp.where(first_core, own[p], far[p])
                m_ref[at + half : at + blk, lanes] = jnp.where(first_core, far[p], own[p])
                o_ref[(2 * r + p) * half : (2 * r + p + 1) * half, lanes] = own[p]
    for k in range(plan.extra):
        at = slice(half + k * piece, half + (k + 1) * piece)
        own, far = own_ref[:, at], far_ref[:, at]
        extra_refs[0][:, 2 * k * piece : (2 * k + 1) * piece] = jnp.where(first_core, own, far)
        extra_refs[0][:, (2 * k + 1) * piece : (2 * k + 2) * piece] = jnp.where(first_core, far, own)
    m = m_ref[...]
    for panel in range(2 * plan.n_row):
        at = slice(panel * half, (panel + 1) * half)
        s = dot(o_ref[at], m)
        s_ref[at] = jnp.where(keep_ref[1, panel : panel + 1] > 0, s, 0.0).astype(jnp.bfloat16)
    for r in range(plan.n_row):
        res = purify(s_ref[2 * r * half : (2 * r + 2) * half], m).astype(jnp.bfloat16)
        for j in range(n_col // 2):
            lanes = slice(2 * j * blk, (2 * j + 2) * blk)
            first, second = split_pair(res[:half, lanes], res[half:, lanes])
            out_ref[r * n_col + 2 * j, blk:] = first
            out_ref[r * n_col + 2 * j + 1, blk:] = second


def extra_block(plan, k, near_ref, far_ref, kept_ref, shift_ref, m_ref, s_ref):
    row_id, col_id = lax.axis_index("row"), lax.axis_index("col")
    blk, n_col = plan.blk, plan.n_col
    even = row_id % 2 == 0
    at = slice(2 * k * plan.piece, (2 * k + 2) * plan.piece)

    def whole(src):
        near, far = near_ref[src, at], far_ref[src, at]
        return jnp.concatenate([jnp.where(even, near, far), jnp.where(even, far, near)], axis=0)

    for r in range(plan.n_row):
        for j in range(n_col // 2):
            lanes = slice(2 * j * blk, (2 * j + 2) * blk)
            pair = split_pair(whole(r * n_col + 2 * j), whole(r * n_col + 2 * j + 1))
            for p in range(2):
                m_ref[(2 * r + p) * blk : (2 * r + p + 1) * blk, lanes] = pair[p]
    for j in range(n_col // 2):
        lanes = slice(2 * j * blk, (2 * j + 2) * blk)
        src = row_id * n_col + 2 * j
        pair = split_pair(whole(src), whole(src + 1))
        for p in range(2):
            s_ref[p * blk : (p + 1) * blk, lanes] = pair[p]
    m = m_ref[...]
    s = dot(s_ref[...], m)
    kept = []
    for p in range(2):
        panel = 2 * row_id + p
        keep = kept_lanes(kept_ref[panel], plan.full + plan.shared + k, shift_ref[panel], blk)
        kept.append(jnp.where(keep > 0, s[p * blk : (p + 1) * blk], 0.0).astype(jnp.bfloat16))
    res = purify(jnp.concatenate(kept, axis=0), m)
    mine = res[:, : 2 * blk]
    for j in range(1, n_col // 2):
        mine = jnp.where(col_id // 2 == j, res[:, 2 * j * blk : (2 * j + 2) * blk], mine)
    first, second = split_pair(mine[:blk], mine[blk:])
    return jnp.where(col_id % 2 == 0, first, second)


def unpack_kernel(plan, kept_hbm, shift_hbm, ret_ref, *refs):
    *halves, out_ref, kept_ref, rows_ref, shift_ref, stage, m_ref, s_ref, sems = refs
    row_id, col_id = lax.axis_index("row"), lax.axis_index("col")
    blk, half, rows = plan.blk, plan.half, plan.back_rows
    copies = [
        pltpu.make_async_copy(shift_hbm, shift_ref, sems.at[0]),
        pltpu.make_async_copy(kept_hbm.at[pl.ds(2 * row_id, 2)], rows_ref, sems.at[1]),
        pltpu.make_async_copy(kept_hbm, kept_ref, sems.at[2]),
    ]
    for copy in copies:
        copy.start()
    for d in range(plan.ndev):
        stage[d * rows : (d + 1) * rows] = ret_ref[d]
    for copy in copies:
        copy.wait()
    for k in range(plan.extra):
        block = extra_block(plan, k, *halves, kept_ref, shift_ref, m_ref, s_ref)
        start = plan.ndev * rows + k * blk
        stage[start : start + blk] = block.astype(jnp.bfloat16)
    for p in range(2):
        shift = shift_ref[2 * row_id + p]
        lanes = slice(p * blk, (p + 1) * blk)
        for e in range(rows_ref.shape[2]):
            u = residue(rows_ref[p, col_id, e], shift)
            for h, start in enumerate(plan.starts(u, rows)):
                tile = stage[pl.ds(start, half), :]
                out_ref[p, h * half : (h + 1) * half, e * blk : (e + 1) * blk] = tile[:, lanes].astype(jnp.float32)


def body(density, density_rows, square_rows, panel_shift):
    both = ("row", "col")
    n_row, n_col = lax.axis_size("row"), lax.axis_size("col")
    blk, rh = density.shape[1], density_rows.shape[2]
    npan = density_rows.shape[0]
    plan = Plan(n_row, n_col, blk)
    ndev, rows, back = plan.ndev, plan.rows, plan.back_rows
    bf16 = jnp.bfloat16
    size = n_col * blk
    square = pltpu.VMEM((size, size), bf16)
    tables = [pltpu.VMEM(square_rows.shape, jnp.int32), pltpu.SMEM((2, npan, rh), jnp.int32), pltpu.SMEM((npan,), jnp.int32)]

    packed, keep = pl.pallas_call(
        functools.partial(pack_kernel, plan),
        out_shape=[
            jax.ShapeDtypeStruct((ndev, rows, 2 * blk), bf16),
            jax.ShapeDtypeStruct((2 if plan.shared else 1, npan, size), jnp.float32),
        ],
        in_specs=[HBM] * 4,
        out_specs=[VMEM] * 2,
        scratch_shapes=[
            pltpu.VMEM(density.shape, bf16),
            tables[1],
            tables[0],
            tables[2],
            pltpu.VMEM((ndev * rows + plan.extra * blk, 2 * blk), bf16),
            pltpu.SemaphoreType.DMA((4,)),
        ],
        compiler_params=PARAMS,
        name="pack",
    )(density, density_rows, square_rows, panel_shift)
    y = lax.all_to_all(packed, both, 0, 0, tiled=True)
    back_shape = jax.ShapeDtypeStruct((ndev, back, 2 * blk), bf16)
    if plan.shared:
        own = y[:, blk:]
        far = lax.ppermute(own, "col", [(i, i ^ 1) for i in range(n_col)])
    out = pl.pallas_call(
        functools.partial(full_kernel, plan),
        out_shape=back_shape,
        in_specs=[VMEM] * 2,
        out_specs=VMEM,
        scratch_shapes=[square] * 2,
        compiler_params=PARAMS,
        cost_estimate=pl.CostEstimate(flops=4 * size**3, bytes_accessed=4 * ndev * rows * 2 * blk, transcendentals=0),
        name="full",
    )(keep, y)
    halves = []
    if plan.shared:
        shapes = [back_shape]
        if plan.extra:
            shapes.append(jax.ShapeDtypeStruct((ndev, 2 * plan.piece * plan.extra, 2 * blk), bf16))
        out, *halves = pl.pallas_call(
            functools.partial(shared_kernel, plan),
            out_shape=shapes,
            in_specs=[VMEM] * 4,
            out_specs=[VMEM] * len(shapes),
            scratch_shapes=[square] + [pltpu.VMEM((size // 2, size), bf16)] * 2,
            compiler_params=PARAMS,
            name="shared",
        )(keep, own, far, out)
    if halves:
        halves.append(lax.ppermute(halves[0], "row", [(i, i ^ 1) for i in range(n_row)]))
    ret = lax.all_to_all(out, both, 0, 0, tiled=True)
    return pl.pallas_call(
        functools.partial(unpack_kernel, plan),
        out_shape=jax.ShapeDtypeStruct(density.shape, jnp.float32),
        in_specs=[HBM] * 2 + [VMEM] * (1 + len(halves)),
        out_specs=VMEM,
        scratch_shapes=tables
        + [
            pltpu.VMEM((ndev * back + plan.extra * blk, 2 * blk), bf16),
            square,
            pltpu.VMEM((2 * blk, size), bf16),
            pltpu.SemaphoreType.DMA((3,)),
        ],
        compiler_params=PARAMS,
        name="unpack",
    )(square_rows, panel_shift, ret, *halves)


def solution(mesh):
    placed = (P("row", None, "col"), P(), P(), P())
    return jax.shard_map(
        body, mesh=mesh, in_specs=placed, out_specs=P("row", None, "col"), check_vma=False
    )
```

```python
import functools

import jax
import jax.numpy as jnp
from jax import lax
from jax.experimental import pallas as pl
from jax.experimental.pallas import tpu as pltpu
from jax.sharding import PartitionSpec as P

PANEL = 49

SMEM = pl.BlockSpec(memory_space=pltpu.SMEM)
VMEM = pl.BlockSpec(memory_space=pltpu.VMEM)
HBM = pl.BlockSpec(memory_space=pltpu.HBM)
PARAMS = pltpu.CompilerParams(vmem_limit_bytes=40 * 1024 * 1024)
PACK_PARAMS = pltpu.CompilerParams(vmem_limit_bytes=63 * 1024 * 1024)


class Plan:
    def __init__(self, n_row, n_col, blk):
        self.n_row, self.n_col, self.blk = n_row, n_col, blk
        self.ndev = n_row * n_col
        chips = self.ndev // 2
        self.full = min(self.ndev, PANEL)
        self.shared = min(chips, PANEL - self.full)
        self.extra = PANEL - self.full - self.shared
        self.half = blk // 2
        self.rows = blk + (self.half if self.shared else 0)

    def starts(self, u):
        rows = self.rows
        first = u * rows
        step = self.half
        if self.shared:
            chip = u - self.full
            is_full, is_shared = u < self.full, u < self.full + self.shared
            tail = self.ndev * rows + (chip - self.shared) * self.blk
            first = jnp.where(is_full, first, jnp.where(is_shared, 2 * chip * rows + self.blk, tail))
            step = jnp.where(jnp.logical_and(is_shared, jnp.logical_not(is_full)), rows, self.half)
        return [pl.multiple_of(first + h * step, self.half) for h in range(2)]

    def slot(self, apart):
        return apart % 2 * (self.n_col // 2) + apart // 2


def residue(row, shift):
    u = row - shift
    return jnp.where(u < 0, u + PANEL, u)


def kept_lanes(rows, u, shift, blk):
    npan = rows.shape[0]
    target = u + shift
    target = jnp.where(target >= PANEL, target - PANEL, target)
    has = jnp.sum((rows == target).astype(jnp.float32), axis=1, keepdims=True)
    lane = lax.broadcasted_iota(jnp.int32, (npan, npan * blk), 1)
    tile = lax.broadcasted_iota(jnp.int32, (npan, npan * blk), 0)
    return jnp.sum(jnp.where(lane // blk == tile, has, 0.0), axis=0, keepdims=True)


def pack_kernel(plan, x_hbm, rows_hbm, shift_hbm, out_ref, *refs):
    *extra_refs, x_ref, rows_ref, shift_ref, stage, sems = refs
    row_id, col_id = lax.axis_index("row"), lax.axis_index("col")
    blk, half, total = plan.blk, plan.half, plan.ndev * plan.rows
    copies = [
        pltpu.make_async_copy(shift_hbm, shift_ref, sems.at[0]),
        pltpu.make_async_copy(rows_hbm.at[pl.ds(2 * row_id, 2)], rows_ref, sems.at[1]),
        pltpu.make_async_copy(x_hbm.at[0], x_ref.at[0], sems.at[2]),
        pltpu.make_async_copy(x_hbm.at[1], x_ref.at[1], sems.at[3]),
    ]
    for copy in copies:
        copy.start()
    stage[...] = jnp.zeros_like(stage)
    for copy in copies[:2]:
        copy.wait()
    for p in range(2):
        copies[2 + p].wait()
        shift = shift_ref[2 * row_id + p]
        lanes = slice(p * blk, (p + 1) * blk)
        for e in range(rows_ref.shape[2]):
            u = residue(rows_ref[p, col_id, e], shift)
            block = x_ref[p, :, e * blk : (e + 1) * blk]
            for h, start in enumerate(plan.starts(u)):
                stage[pl.ds(start, half), lanes] = block[h * half : (h + 1) * half]
    copies = [pltpu.make_async_copy(stage.at[pl.ds(0, total)], out_ref, sems.at[0])]
    for ref in extra_refs:
        copies.append(pltpu.make_async_copy(stage.at[pl.ds(total, plan.extra * blk)], ref, sems.at[1]))
    for copy in copies:
        copy.start()
    for copy in copies:
        copy.wait()


def mask_kernel(plan, shift_ref, kept_ref, keep_ref):
    me = lax.axis_index("row") * plan.n_col + lax.axis_index("col")
    sets = [jnp.minimum(me, plan.full - 1), plan.full + me // 2]
    sets += [plan.full + plan.shared + k for k in range(plan.extra)]
    for k, u in enumerate(sets[: keep_ref.shape[0]]):
        for panel in range(2 * plan.n_row):
            keep_ref[k, panel : panel + 1] = kept_lanes(kept_ref[panel], u, shift_ref[panel], plan.blk)


def split_pair(low, high):
    blk = low.shape[1] // 2
    first = jnp.concatenate([low[:, :blk], high[:, :blk]], axis=1)
    second = jnp.concatenate([low[:, blk:], high[:, blk:]], axis=1)
    return first, second


def dot(a, b):
    return jnp.dot(a, b, preferred_element_type=jnp.float32)


def purify(s, m):
    return 3.0 * s.astype(jnp.float32) - 2.0 * dot(s, m)


def full_kernel(plan, keep_ref, y_ref, out_ref, m_ref, s_ref):
    blk, n_col = plan.blk, plan.n_col
    for r in range(plan.n_row):
        for j in range(n_col // 2):
            src = r * n_col + 2 * j
            first, second = split_pair(y_ref[src, :blk], y_ref[src + 1, :blk])
            lanes = slice(2 * j * blk, (2 * j + 2) * blk)
            m_ref[2 * r * blk : (2 * r + 1) * blk, lanes] = first
            m_ref[(2 * r + 1) * blk : (2 * r + 2) * blk, lanes] = second
    m = m_ref[...]
    for panel in range(2 * plan.n_row):
        at = slice(panel * blk, (panel + 1) * blk)
        s = dot(m_ref[at], m)
        s_ref[at] = jnp.where(keep_ref[0, panel : panel + 1] > 0, s, 0.0).astype(jnp.bfloat16)
    for r in range(plan.n_row):
        res = purify(s_ref[2 * r * blk : (2 * r + 2) * blk], m).astype(jnp.bfloat16)
        for j in range(n_col // 2):
            lanes = slice(2 * j * blk, (2 * j + 2) * blk)
            first, second = split_pair(res[:blk, lanes], res[blk:, lanes])
            out_ref[r * n_col + 2 * j, :blk] = first
            out_ref[r * n_col + 2 * j + 1, :blk] = second


def shared_kernel(plan, keep_ref, own_ref, far_ref, part_ref, out_ref, m_ref, s_ref, o_ref):
    blk, half, n_col = plan.blk, plan.half, plan.n_col
    first_core = lax.axis_index("col") % 2 == 0
    out_ref[:, :blk] = part_ref[:, :blk]
    for r in range(plan.n_row):
        for j in range(n_col // 2):
            src = r * n_col + 2 * j
            lanes = slice(2 * j * blk, (2 * j + 2) * blk)
            own = split_pair(own_ref[src], own_ref[src + 1])
            far = split_pair(far_ref[src], far_ref[src + 1])
            for p in range(2):
                at = (2 * r + p) * blk
                m_ref[at : at + half, lanes] = jnp.where(first_core, own[p], far[p])
                m_ref[at + half : at + blk, lanes] = jnp.where(first_core, far[p], own[p])
                o_ref[(2 * r + p) * half : (2 * r + p + 1) * half, lanes] = own[p]
    m = m_ref[...]
    for panel in range(2 * plan.n_row):
        at = slice(panel * half, (panel + 1) * half)
        s = dot(o_ref[at], m)
        s_ref[at] = jnp.where(keep_ref[1, panel : panel + 1] > 0, s, 0.0).astype(jnp.bfloat16)
    for r in range(plan.n_row):
        res = purify(s_ref[2 * r * half : (2 * r + 2) * half], m).astype(jnp.bfloat16)
        for j in range(n_col // 2):
            lanes = slice(2 * j * blk, (2 * j + 2) * blk)
            first, second = split_pair(res[:half, lanes], res[half:, lanes])
            out_ref[r * n_col + 2 * j, blk:] = first
            out_ref[r * n_col + 2 * j + 1, blk:] = second


def extra_kernel(plan, keep_ref, *refs):
    row_refs, (out_ref, m_ref, o_ref) = refs[: plan.n_row], refs[plan.n_row :]
    row_id, col_id = lax.axis_index("row"), lax.axis_index("col")
    blk, n_col = plan.blk, plan.n_col
    for k in range(plan.extra):
        at = slice(k * blk, (k + 1) * blk)
        for apart, ref in enumerate(row_refs):
            start = pl.multiple_of(jnp.bitwise_xor(row_id, apart) * 2 * blk, 2 * blk)
            for j in range(n_col // 2):
                lanes = slice(2 * j * blk, (2 * j + 2) * blk)
                low, high = (ref[plan.slot(jnp.bitwise_xor(col_id, 2 * j + c)), at] for c in range(2))
                tile = jnp.concatenate(split_pair(low, high), axis=0)
                m_ref[pl.ds(start, 2 * blk), lanes] = tile
                if apart == 0:
                    o_ref[:, lanes] = tile
        m = m_ref[...]
        s = dot(o_ref[...], m)
        kept = []
        for p in range(2):
            keep = keep_ref[2 + k, pl.ds(2 * row_id + p, 1)]
            kept.append(jnp.where(keep > 0, s[p * blk : (p + 1) * blk], 0.0).astype(jnp.bfloat16))
        res = purify(jnp.concatenate(kept, axis=0), m)
        mine = res[:, : 2 * blk]
        for j in range(1, n_col // 2):
            mine = jnp.where(col_id // 2 == j, res[:, 2 * j * blk : (2 * j + 2) * blk], mine)
        first, second = split_pair(mine[:blk], mine[blk:])
        out_ref[at] = jnp.where(col_id % 2 == 0, first, second).astype(jnp.bfloat16)


def unpack_kernel(plan, kept_hbm, shift_hbm, ret_ref, *refs):
    *extra_refs, out_ref, rows_ref, shift_ref, stage, sems = refs
    row_id, col_id = lax.axis_index("row"), lax.axis_index("col")
    blk, half, rows, ndev = plan.blk, plan.half, plan.rows, plan.ndev
    copies = [
        pltpu.make_async_copy(shift_hbm, shift_ref, sems.at[0]),
        pltpu.make_async_copy(kept_hbm.at[pl.ds(2 * row_id, 2)], rows_ref, sems.at[1]),
    ]
    for copy in copies:
        copy.start()
    for d in range(ndev):
        stage[d * rows : (d + 1) * rows] = ret_ref[d]
    for ref in extra_refs:
        stage[ndev * rows :] = ref[...]
    for copy in copies:
        copy.wait()
    for p in range(2):
        shift = shift_ref[2 * row_id + p]
        lanes = slice(p * blk, (p + 1) * blk)
        for e in range(rows_ref.shape[2]):
            u = residue(rows_ref[p, col_id, e], shift)
            for h, start in enumerate(plan.starts(u)):
                tile = stage[pl.ds(start, half), :]
                out_ref[p, h * half : (h + 1) * half, e * blk : (e + 1) * blk] = tile[:, lanes].astype(jnp.float32)


def swapped(shard, axis, by):
    return lax.ppermute(shard, axis, [(i, i ^ by) for i in range(lax.axis_size(axis))])


def body(density, density_rows, square_rows, panel_shift):
    both = ("row", "col")
    n_row, n_col = lax.axis_size("row"), lax.axis_size("col")
    blk, rh = density.shape[1], density_rows.shape[2]
    npan = density_rows.shape[0]
    plan = Plan(n_row, n_col, blk)
    ndev, rows = plan.ndev, plan.rows
    bf16 = jnp.bfloat16
    size = n_col * blk
    square = pltpu.VMEM((size, size), bf16)
    tables = [pltpu.SMEM((2, npan, rh), jnp.int32), pltpu.SMEM((npan,), jnp.int32)]
    stage = pltpu.VMEM((ndev * rows + plan.extra * blk, 2 * blk), bf16)
    moved = jax.ShapeDtypeStruct((ndev, rows, 2 * blk), bf16)

    flat = jax.ShapeDtypeStruct((ndev * rows, 2 * blk), bf16)
    extra_shapes = [jax.ShapeDtypeStruct((plan.extra * blk, 2 * blk), bf16)] if plan.extra else []
    packed, *extra = pl.pallas_call(
        functools.partial(pack_kernel, plan),
        out_shape=[flat] + extra_shapes,
        in_specs=[HBM] * 3,
        out_specs=[HBM] * (1 + len(extra_shapes)),
        scratch_shapes=[pltpu.VMEM(density.shape, bf16)] + tables + [stage, pltpu.SemaphoreType.DMA((4,))],
        compiler_params=PACK_PARAMS,
        name="pack",
    )(density, density_rows, panel_shift)
    y = lax.all_to_all(packed.reshape(moved.shape), both, 0, 0, tiled=True)
    sets = 1 + (1 if plan.shared else 0) + plan.extra
    keep = pl.pallas_call(
        functools.partial(mask_kernel, plan),
        out_shape=jax.ShapeDtypeStruct((sets, npan, size), jnp.float32),
        in_specs=[SMEM, VMEM],
        out_specs=VMEM,
        compiler_params=PARAMS,
        name="masks",
    )(panel_shift, square_rows)
    if plan.extra:
        extra = extra[0][None]
        line = [extra] + [swapped(extra, "col", by) for by in range(2, n_col, 2)]
        y, keep, *line = lax.optimization_barrier((y, keep, *line))
        line = jnp.concatenate(line, axis=0)
        line = jnp.concatenate([line, swapped(line, "col", 1)], axis=0)
        plane = [line] + [swapped(line, "row", by) for by in range(1, n_row)]
        extra = [
            pl.pallas_call(
                functools.partial(extra_kernel, plan),
                out_shape=extra_shapes[0],
                in_specs=[VMEM] * (1 + n_row),
                out_specs=VMEM,
                scratch_shapes=[square, pltpu.VMEM((2 * blk, size), bf16)],
                compiler_params=PARAMS,
                name="extra",
            )(keep, *plane)
        ]
    if plan.shared:
        own = y[:, blk:]
        far = swapped(own, "col", 1)
    out = pl.pallas_call(
        functools.partial(full_kernel, plan),
        out_shape=moved,
        in_specs=[VMEM] * 2,
        out_specs=VMEM,
        scratch_shapes=[square] * 2,
        compiler_params=PARAMS,
        cost_estimate=pl.CostEstimate(flops=4 * size**3, bytes_accessed=4 * ndev * rows * 2 * blk, transcendentals=0),
        name="full",
    )(keep, y)
    if plan.shared:
        out = pl.pallas_call(
            functools.partial(shared_kernel, plan),
            out_shape=moved,
            in_specs=[VMEM] * 4,
            out_specs=VMEM,
            scratch_shapes=[square] + [pltpu.VMEM((size // 2, size), bf16)] * 2,
            compiler_params=PARAMS,
            name="shared",
        )(keep, own, far, out)
    ret = lax.all_to_all(out, both, 0, 0, tiled=True)
    return pl.pallas_call(
        functools.partial(unpack_kernel, plan),
        out_shape=jax.ShapeDtypeStruct(density.shape, jnp.float32),
        in_specs=[HBM] * 2 + [VMEM] * (1 + len(extra)),
        out_specs=VMEM,
        scratch_shapes=tables + [stage, pltpu.SemaphoreType.DMA((2,))],
        compiler_params=PARAMS,
        name="unpack",
    )(square_rows, panel_shift, ret, *extra)


def solution(mesh):
    placed = (P("row", None, "col"), P(), P(), P())
    return jax.shard_map(
        body, mesh=mesh, in_specs=placed, out_specs=P("row", None, "col"), check_vma=False
    )
```

```python
import functools

import jax
import jax.numpy as jnp
import numpy as np
from jax import lax
from jax.experimental import pallas as pl
from jax.experimental.pallas import tpu as pltpu
from jax.sharding import PartitionSpec as P

PANEL = 49

SMEM = pl.BlockSpec(memory_space=pltpu.SMEM)
VMEM = pl.BlockSpec(memory_space=pltpu.VMEM)
HBM = pl.BlockSpec(memory_space=pltpu.HBM)
PARAMS = pltpu.CompilerParams(vmem_limit_bytes=40 * 1024 * 1024)
PACK_PARAMS = pltpu.CompilerParams(vmem_limit_bytes=63 * 1024 * 1024)


class Plan:
    def __init__(self, n_row, n_col, blk):
        self.n_row, self.n_col, self.blk = n_row, n_col, blk
        self.ndev = n_row * n_col
        chips = self.ndev // 2
        self.full = min(self.ndev, PANEL)
        self.shared = min(chips, PANEL - self.full)
        self.extra = PANEL - self.full - self.shared
        self.half = blk // 2
        self.rows = blk + (self.half if self.shared else 0)

    def starts(self):
        table = np.zeros((2, 2 * PANEL - 1), np.int32)
        for i in range(2 * PANEL - 1):
            u = (i + 1) % PANEL
            chip = u - self.full
            if u < self.full:
                first, step = u * self.rows, self.half
            elif chip < self.shared:
                first, step = 2 * chip * self.rows + self.blk, self.rows
            else:
                first, step = self.ndev * self.rows + (chip - self.shared) * self.blk, self.half
            table[:, i] = first, first + step
        return table

    def slot(self, apart):
        return apart % 2 * (self.n_col // 2) + apart // 2


def kept_lanes(rows, u, shift, blk):
    npan = rows.shape[0]
    target = u + shift
    target = jnp.where(target >= PANEL, target - PANEL, target)
    has = jnp.sum((rows == target).astype(jnp.float32), axis=1, keepdims=True)
    lane = lax.broadcasted_iota(jnp.int32, (npan, npan * blk), 1)
    tile = lax.broadcasted_iota(jnp.int32, (npan, npan * blk), 0)
    return jnp.sum(jnp.where(lane // blk == tile, has, 0.0), axis=0, keepdims=True)


def pack_kernel(plan, x_hbm, rows_hbm, shift_hbm, starts_hbm, out_ref, *refs):
    *extra_refs, x_ref, rows_ref, shift_ref, starts_ref, stage, sems = refs
    row_id, col_id = lax.axis_index("row"), lax.axis_index("col")
    blk, half, total = plan.blk, plan.half, plan.ndev * plan.rows
    copies = [
        pltpu.make_async_copy(shift_hbm, shift_ref, sems.at[0]),
        pltpu.make_async_copy(rows_hbm.at[pl.ds(2 * row_id, 2)], rows_ref, sems.at[1]),
        pltpu.make_async_copy(starts_hbm, starts_ref, sems.at[2]),
        pltpu.make_async_copy(x_hbm.at[0], x_ref.at[0], sems.at[3]),
        pltpu.make_async_copy(x_hbm.at[1], x_ref.at[1], sems.at[4]),
    ]
    for copy in copies:
        copy.start()
    stage[...] = jnp.zeros_like(stage)
    for copy in copies[:3]:
        copy.wait()
    for p in range(2):
        copies[3 + p].wait()
        base = PANEL - 1 - shift_ref[2 * row_id + p]
        lanes = slice(p * blk, (p + 1) * blk)
        for e in range(rows_ref.shape[2]):
            at = rows_ref[p, col_id, e] + base
            block = x_ref[p, :, e * blk : (e + 1) * blk]
            for h in range(2):
                start = pl.multiple_of(starts_ref[h, at], half)
                stage[pl.ds(start, half), lanes] = block[h * half : (h + 1) * half]
    copies = [pltpu.make_async_copy(stage.at[pl.ds(0, total)], out_ref, sems.at[0])]
    for ref in extra_refs:
        copies.append(pltpu.make_async_copy(stage.at[pl.ds(total, plan.extra * blk)], ref, sems.at[1]))
    for copy in copies:
        copy.start()
    for copy in copies:
        copy.wait()


def mask_kernel(plan, shift_ref, kept_ref, keep_ref):
    me = lax.axis_index("row") * plan.n_col + lax.axis_index("col")
    sets = [jnp.minimum(me, plan.full - 1), plan.full + me // 2]
    sets += [plan.full + plan.shared + k for k in range(plan.extra)]
    for k, u in enumerate(sets[: keep_ref.shape[0]]):
        for panel in range(2 * plan.n_row):
            keep_ref[k, panel : panel + 1] = kept_lanes(kept_ref[panel], u, shift_ref[panel], plan.blk)


def split_pair(low, high):
    blk = low.shape[1] // 2
    first = jnp.concatenate([low[:, :blk], high[:, :blk]], axis=1)
    second = jnp.concatenate([low[:, blk:], high[:, blk:]], axis=1)
    return first, second


def dot(a, b):
    return jnp.dot(a, b, preferred_element_type=jnp.float32)


def purify(s, m):
    return 3.0 * s.astype(jnp.float32) - 2.0 * dot(s, m)


def put_blocks(plan, res, height, out_ref):
    for r in range(plan.n_row):
        for j in range(plan.n_col // 2):
            lanes = slice(2 * j * plan.blk, (2 * j + 2) * plan.blk)
            upper = res[2 * r * height : (2 * r + 1) * height, lanes]
            lower = res[(2 * r + 1) * height : (2 * r + 2) * height, lanes]
            to = r * plan.n_col + 2 * j
            out_ref[to], out_ref[to + 1] = split_pair(upper, lower)


def full_kernel(plan, keep_ref, y_ref, out_ref, m_ref, s_ref):
    blk, n_col = plan.blk, plan.n_col
    for r in range(plan.n_row):
        for j in range(n_col // 2):
            src = r * n_col + 2 * j
            first, second = split_pair(y_ref[src, :blk], y_ref[src + 1, :blk])
            lanes = slice(2 * j * blk, (2 * j + 2) * blk)
            m_ref[2 * r * blk : (2 * r + 1) * blk, lanes] = first
            m_ref[(2 * r + 1) * blk : (2 * r + 2) * blk, lanes] = second
    m = m_ref[...]
    s = dot(m, m)
    for panel in range(2 * plan.n_row):
        at = slice(panel * blk, (panel + 1) * blk)
        s_ref[at] = jnp.where(keep_ref[0, panel : panel + 1] > 0, s[at], 0.0).astype(jnp.bfloat16)
    res = purify(s_ref[...], m).astype(jnp.bfloat16)
    put_blocks(plan, res, blk, out_ref)


def shared_kernel(plan, keep_ref, own_ref, far_ref, part_ref, out_hbm, m_ref, s_ref, o_ref, res_ref, sems):
    blk, half, n_col = plan.blk, plan.half, plan.n_col
    first_core = lax.axis_index("col") % 2 == 0
    part_copy = pltpu.make_async_copy(part_ref, out_hbm.at[:, pl.ds(0, blk)], sems.at[0])
    part_copy.start()
    for r in range(plan.n_row):
        for j in range(n_col // 2):
            src = r * n_col + 2 * j
            lanes = slice(2 * j * blk, (2 * j + 2) * blk)
            own = split_pair(own_ref[src], own_ref[src + 1])
            far = split_pair(far_ref[src], far_ref[src + 1])
            for p in range(2):
                at = (2 * r + p) * blk
                m_ref[at : at + half, lanes] = jnp.where(first_core, own[p], far[p])
                m_ref[at + half : at + blk, lanes] = jnp.where(first_core, far[p], own[p])
                o_ref[(2 * r + p) * half : (2 * r + p + 1) * half, lanes] = own[p]
    m = m_ref[...]
    s = dot(o_ref[...], m)
    for panel in range(2 * plan.n_row):
        at = slice(panel * half, (panel + 1) * half)
        s_ref[at] = jnp.where(keep_ref[1, panel : panel + 1] > 0, s[at], 0.0).astype(jnp.bfloat16)
    put_blocks(plan, purify(s_ref[...], m).astype(jnp.bfloat16), half, res_ref)
    res_copy = pltpu.make_async_copy(res_ref, out_hbm.at[:, pl.ds(blk, half)], sems.at[1])
    res_copy.start()
    part_copy.wait()
    res_copy.wait()


def extra_kernel(plan, keep_ref, *refs):
    row_refs, (out_ref, m_ref, o_ref) = refs[: plan.n_row], refs[plan.n_row :]
    row_id, col_id = lax.axis_index("row"), lax.axis_index("col")
    blk, n_col = plan.blk, plan.n_col
    for k in range(plan.extra):
        at = slice(k * blk, (k + 1) * blk)
        for apart, ref in enumerate(row_refs):
            start = pl.multiple_of(jnp.bitwise_xor(row_id, apart) * 2 * blk, 2 * blk)
            for j in range(n_col // 2):
                lanes = slice(2 * j * blk, (2 * j + 2) * blk)
                low, high = (ref[plan.slot(jnp.bitwise_xor(col_id, 2 * j + c)), at] for c in range(2))
                tile = jnp.concatenate(split_pair(low, high), axis=0)
                m_ref[pl.ds(start, 2 * blk), lanes] = tile
                if apart == 0:
                    o_ref[:, lanes] = tile
        m = m_ref[...]
        s = dot(o_ref[...], m)
        kept = []
        for p in range(2):
            keep = keep_ref[2 + k, pl.ds(2 * row_id + p, 1)]
            kept.append(jnp.where(keep > 0, s[p * blk : (p + 1) * blk], 0.0).astype(jnp.bfloat16))
        res = purify(jnp.concatenate(kept, axis=0), m)
        mine = res[:, : 2 * blk]
        for j in range(1, n_col // 2):
            mine = jnp.where(col_id // 2 == j, res[:, 2 * j * blk : (2 * j + 2) * blk], mine)
        first, second = split_pair(mine[:blk], mine[blk:])
        out_ref[at] = jnp.where(col_id % 2 == 0, first, second).astype(jnp.bfloat16)


def unpack_kernel(plan, kept_hbm, shift_hbm, starts_hbm, ret_ref, *refs):
    *extra_refs, out_hbm, rows_ref, shift_ref, starts_ref, stage, out_ref, sems = refs
    row_id, col_id = lax.axis_index("row"), lax.axis_index("col")
    blk, half, total = plan.blk, plan.half, plan.ndev * plan.rows
    copies = [
        pltpu.make_async_copy(shift_hbm, shift_ref, sems.at[0]),
        pltpu.make_async_copy(kept_hbm.at[pl.ds(2 * row_id, 2)], rows_ref, sems.at[1]),
        pltpu.make_async_copy(starts_hbm, starts_ref, sems.at[2]),
    ]
    for copy in copies:
        copy.start()
    stage[:total] = ret_ref[...]
    for ref in extra_refs:
        stage[total:] = ref[...]
    for copy in copies:
        copy.wait()
    copies = [pltpu.make_async_copy(out_ref.at[p], out_hbm.at[p], sems.at[3 + p]) for p in range(2)]
    for p in range(2):
        base = PANEL - 1 - shift_ref[2 * row_id + p]
        lanes = slice(p * blk, (p + 1) * blk)
        for e in range(rows_ref.shape[2]):
            at = rows_ref[p, col_id, e] + base
            for h in range(2):
                tile = stage[pl.ds(pl.multiple_of(starts_ref[h, at], half), half), :]
                out_ref[p, h * half : (h + 1) * half, e * blk : (e + 1) * blk] = tile[:, lanes].astype(jnp.float32)
        copies[p].start()
    for copy in copies:
        copy.wait()


def swapped(shard, axis, by):
    return lax.ppermute(shard, axis, [(i, i ^ by) for i in range(lax.axis_size(axis))])


def body(density, density_rows, square_rows, panel_shift):
    both = ("row", "col")
    n_row, n_col = lax.axis_size("row"), lax.axis_size("col")
    blk, rh = density.shape[1], density_rows.shape[2]
    npan = density_rows.shape[0]
    plan = Plan(n_row, n_col, blk)
    ndev, rows = plan.ndev, plan.rows
    bf16 = jnp.bfloat16
    size = n_col * blk
    square = pltpu.VMEM((size, size), bf16)
    tables = [pltpu.SMEM((2, npan, rh), jnp.int32), pltpu.SMEM((npan,), jnp.int32)]
    starts = jnp.asarray(plan.starts())
    tables.append(pltpu.SMEM(starts.shape, jnp.int32))
    stage = pltpu.VMEM((ndev * rows + plan.extra * blk, 2 * blk), bf16)
    moved = jax.ShapeDtypeStruct((ndev, rows, 2 * blk), bf16)

    flat = jax.ShapeDtypeStruct((ndev * rows, 2 * blk), bf16)
    extra_shapes = [jax.ShapeDtypeStruct((plan.extra * blk, 2 * blk), bf16)] if plan.extra else []
    packed, *extra = pl.pallas_call(
        functools.partial(pack_kernel, plan),
        out_shape=[flat] + extra_shapes,
        in_specs=[HBM] * 4,
        out_specs=[HBM] * (1 + len(extra_shapes)),
        scratch_shapes=[pltpu.VMEM(density.shape, bf16)] + tables + [stage, pltpu.SemaphoreType.DMA((5,))],
        compiler_params=PACK_PARAMS,
        name="pack",
    )(density, density_rows, panel_shift, starts)
    y = lax.all_to_all(packed.reshape(moved.shape), both, 0, 0, tiled=True)
    sets = 1 + (1 if plan.shared else 0) + plan.extra
    keep = pl.pallas_call(
        functools.partial(mask_kernel, plan),
        out_shape=jax.ShapeDtypeStruct((sets, npan, size), jnp.float32),
        in_specs=[SMEM, VMEM],
        out_specs=VMEM,
        compiler_params=PARAMS,
        name="masks",
    )(panel_shift, square_rows)
    if plan.extra:
        extra = extra[0][None]
        line = [extra] + [swapped(extra, "col", by) for by in range(2, n_col, 2)]
        y, keep, *line = lax.optimization_barrier((y, keep, *line))
        line = jnp.concatenate(line, axis=0)
        line = jnp.concatenate([line, swapped(line, "col", 1)], axis=0)
        plane = [line] + [swapped(line, "row", by) for by in range(1, n_row)]
        extra = [
            pl.pallas_call(
                functools.partial(extra_kernel, plan),
                out_shape=extra_shapes[0],
                in_specs=[VMEM] * (1 + n_row),
                out_specs=VMEM,
                scratch_shapes=[square, pltpu.VMEM((2 * blk, size), bf16)],
                compiler_params=PARAMS,
                name="extra",
            )(keep, *plane)
        ]
    if plan.shared:
        own = y[:, blk:]
        far = swapped(own, "col", 1)
    out = pl.pallas_call(
        functools.partial(full_kernel, plan),
        out_shape=jax.ShapeDtypeStruct((ndev, blk, 2 * blk), bf16),
        in_specs=[VMEM] * 2,
        out_specs=VMEM,
        scratch_shapes=[square] * 2,
        compiler_params=PARAMS,
        cost_estimate=pl.CostEstimate(flops=4 * size**3, bytes_accessed=4 * ndev * rows * 2 * blk, transcendentals=0),
        name="full",
    )(keep, y)
    if plan.shared:
        out = pl.pallas_call(
            functools.partial(shared_kernel, plan),
            out_shape=moved,
            in_specs=[VMEM] * 4,
            out_specs=HBM,
            scratch_shapes=[square]
            + [pltpu.VMEM((size // 2, size), bf16)] * 2
            + [pltpu.VMEM((ndev, plan.half, 2 * blk), bf16), pltpu.SemaphoreType.DMA((2,))],
            compiler_params=PARAMS,
            name="shared",
        )(keep, own, far, out)
    ret = lax.all_to_all(out, both, 0, 0, tiled=True)
    return pl.pallas_call(
        functools.partial(unpack_kernel, plan),
        out_shape=jax.ShapeDtypeStruct(density.shape, jnp.float32),
        in_specs=[HBM] * 3 + [VMEM] * (1 + len(extra)),
        out_specs=HBM,
        scratch_shapes=tables + [stage, pltpu.VMEM(density.shape, jnp.float32), pltpu.SemaphoreType.DMA((5,))],
        compiler_params=PARAMS,
        name="unpack",
    )(square_rows, panel_shift, starts, ret.reshape(flat.shape), *extra)


def solution(mesh):
    placed = (P("row", None, "col"), P(), P(), P())
    return jax.shard_map(
        body, mesh=mesh, in_specs=placed, out_specs=P("row", None, "col"), check_vma=False
    )
```

```python
import functools

import jax
import jax.numpy as jnp
import numpy as np
from jax import lax
from jax.experimental import pallas as pl
from jax.experimental.pallas import tpu as pltpu
from jax.sharding import PartitionSpec as P

PANEL = 49

SMEM = pl.BlockSpec(memory_space=pltpu.SMEM)
VMEM = pl.BlockSpec(memory_space=pltpu.VMEM)
HBM = pl.BlockSpec(memory_space=pltpu.HBM)
PARAMS = pltpu.CompilerParams(vmem_limit_bytes=40 * 1024 * 1024)
PACK_PARAMS = pltpu.CompilerParams(vmem_limit_bytes=63 * 1024 * 1024)


class Plan:
    def __init__(self, n_row, n_col, blk):
        self.n_row, self.n_col, self.blk = n_row, n_col, blk
        self.ndev = n_row * n_col
        self.line = n_col // 2
        chips = self.ndev // 2
        self.full = min(self.ndev, PANEL)
        self.shared = min(chips, PANEL - self.full)
        self.extra = PANEL - self.full - self.shared
        self.half = blk // 2
        self.rows = blk + (self.half if self.shared else 0)
        self.slots = self.n_row + self.extra if self.shared else 0

    def send_slot(self, at, chip):
        u = jnp.where(at < PANEL - 1, at + 1, at + 1 - PANEL)
        if not self.shared:
            return u
        apart = jnp.bitwise_xor(u - self.full, chip)
        shift = self.line.bit_length() - 1
        plane, line = jnp.right_shift(apart, shift), jnp.bitwise_and(apart, self.line - 1)
        beyond = u - self.full - self.shared
        slot = jnp.where(beyond < 0, line * self.slots + plane, self.n_row + beyond)
        return jnp.where(u < self.full, u, self.ndev + slot)

    def starts(self):
        table = np.zeros((2, 2 * PANEL - 1), np.int32)
        for i in range(2 * PANEL - 1):
            u = (i + 1) % PANEL
            chip = u - self.full
            if u < self.full:
                first, step = u * self.rows, self.half
            elif chip < self.shared:
                first, step = 2 * chip * self.rows + self.blk, self.rows
            else:
                first, step = self.ndev * self.rows + (chip - self.shared) * self.blk, self.half
            table[:, i] = first, first + step
        return table

    def slot(self, apart):
        return apart % 2 * self.line + apart // 2


def kept_lanes(rows, u, shift, blk):
    npan = rows.shape[0]
    target = u + shift
    target = jnp.where(target >= PANEL, target - PANEL, target)
    has = jnp.sum((rows == target).astype(jnp.float32), axis=1, keepdims=True)
    lane = lax.broadcasted_iota(jnp.int32, (npan, npan * blk), 1)
    tile = lax.broadcasted_iota(jnp.int32, (npan, npan * blk), 0)
    return jnp.sum(jnp.where(lane // blk == tile, has, 0.0), axis=0, keepdims=True)


def pack_kernel(plan, x_hbm, rows_hbm, shift_hbm, *refs):
    *out_refs, x_ref, rows_ref, shift_ref, stage, sems = refs
    row_id, col_id = lax.axis_index("row"), lax.axis_index("col")
    blk, ndev, slots = plan.blk, plan.ndev, plan.slots
    chip = row_id * plan.line + col_id // 2
    copies = [
        pltpu.make_async_copy(shift_hbm, shift_ref, sems.at[0]),
        pltpu.make_async_copy(rows_hbm.at[pl.ds(2 * row_id, 2)], rows_ref, sems.at[1]),
        pltpu.make_async_copy(x_hbm.at[0], x_ref.at[0], sems.at[2]),
        pltpu.make_async_copy(x_hbm.at[1], x_ref.at[1], sems.at[3]),
    ]
    for copy in copies:
        copy.start()
    stage[...] = jnp.zeros_like(stage)
    for copy in copies[:2]:
        copy.wait()
    for p in range(2):
        copies[2 + p].wait()
        base = PANEL - 1 - shift_ref[2 * row_id + p]
        lanes = slice(p * blk, (p + 1) * blk)
        for e in range(rows_ref.shape[2]):
            slot = plan.send_slot(rows_ref[p, col_id, e] + base, chip)
            stage[slot, :, lanes] = x_ref[p, :, e * blk : (e + 1) * blk]
    for k in range(plan.extra):
        block = stage[ndev + plan.n_row + k]
        for i in range(1, plan.line):
            stage[ndev + i * slots + plan.n_row + k] = block
    spans = [(0, ndev)] + [(ndev + i * slots, slots) for i in range(len(out_refs) - 1)]
    copies = [
        pltpu.make_async_copy(stage.at[pl.ds(first, size)], ref, sems.at[i])
        for i, ((first, size), ref) in enumerate(zip(spans, out_refs))
    ]
    for copy in copies:
        copy.start()
    for copy in copies:
        copy.wait()


def mask_kernel(plan, shift_ref, kept_ref, keep_ref):
    me = lax.axis_index("row") * plan.n_col + lax.axis_index("col")
    sets = [jnp.minimum(me, plan.full - 1), plan.full + me // 2]
    sets += [plan.full + plan.shared + k for k in range(plan.extra)]
    for k, u in enumerate(sets[: keep_ref.shape[0]]):
        for panel in range(2 * plan.n_row):
            keep_ref[k, panel : panel + 1] = kept_lanes(kept_ref[panel], u, shift_ref[panel], plan.blk)


def split_pair(low, high):
    blk = low.shape[1] // 2
    first = jnp.concatenate([low[:, :blk], high[:, :blk]], axis=1)
    second = jnp.concatenate([low[:, blk:], high[:, blk:]], axis=1)
    return first, second


def dot(a, b):
    return jnp.dot(a, b, preferred_element_type=jnp.float32)


def purify(s, m):
    return 3.0 * s.astype(jnp.float32) - 2.0 * dot(s, m)


def put_blocks(plan, res, height, out_ref):
    for r in range(plan.n_row):
        for j in range(plan.n_col // 2):
            lanes = slice(2 * j * plan.blk, (2 * j + 2) * plan.blk)
            upper = res[2 * r * height : (2 * r + 1) * height, lanes]
            lower = res[(2 * r + 1) * height : (2 * r + 2) * height, lanes]
            to = r * plan.n_col + 2 * j
            out_ref[to], out_ref[to + 1] = split_pair(upper, lower)


def full_kernel(plan, keep_ref, y_ref, *refs):
    *shared_refs, out_hbm, m_ref, s_ref, res_ref, sems = refs
    blk, n_col = plan.blk, plan.n_col
    copies = [
        pltpu.make_async_copy(ref, out_hbm.at[:, pl.ds(blk, plan.half)], sems.at[1]) for ref in shared_refs
    ]
    for copy in copies:
        copy.start()
    for r in range(plan.n_row):
        for j in range(n_col // 2):
            src = r * n_col + 2 * j
            first, second = split_pair(y_ref[src], y_ref[src + 1])
            lanes = slice(2 * j * blk, (2 * j + 2) * blk)
            m_ref[2 * r * blk : (2 * r + 1) * blk, lanes] = first
            m_ref[(2 * r + 1) * blk : (2 * r + 2) * blk, lanes] = second
    m = m_ref[...]
    s = dot(m, m)
    for panel in range(2 * plan.n_row):
        at = slice(panel * blk, (panel + 1) * blk)
        s_ref[at] = jnp.where(keep_ref[0, panel : panel + 1] > 0, s[at], 0.0).astype(jnp.bfloat16)
    put_blocks(plan, purify(s_ref[...], m).astype(jnp.bfloat16), blk, res_ref)
    copies.append(pltpu.make_async_copy(res_ref, out_hbm.at[:, pl.ds(0, blk)], sems.at[0]))
    copies[-1].start()
    for copy in copies:
        copy.wait()


def regroup_kernel(plan, *refs):
    line, plane, extra = refs[: plan.line], refs[plan.line : plan.line + plan.n_row], refs[plan.line + plan.n_row :]
    for i, sent in enumerate(line):
        for r, ref in enumerate(plane):
            ref[i] = sent[r]
        for ref in extra:
            for k in range(plan.extra):
                ref[k * plan.line + i] = sent[plan.n_row + k]


def shared_kernel(plan, keep_ref, own_ref, far_ref, out_ref, m_ref, s_ref, o_ref):
    n_row, n_col, blk, half = plan.n_row, plan.n_col, plan.blk, plan.half
    row_id, col_id = lax.axis_index("row"), lax.axis_index("col")
    first_core = col_id % 2 == 0
    for r in range(n_row):
        panel = 2 * jnp.bitwise_xor(row_id, r)
        start = pl.multiple_of(panel * blk, 2 * blk)
        for j in range(n_col // 2):
            lanes = slice(2 * j * blk, (2 * j + 2) * blk)
            at = r * plan.line + jnp.bitwise_xor(col_id // 2, j)
            own, far = own_ref[at], far_ref[at]
            pair = split_pair(jnp.where(first_core, own, far), jnp.where(first_core, far, own))
            m_ref[pl.ds(start, 2 * blk), lanes] = jnp.concatenate(pair, axis=0)
            for p in range(2):
                at = slice((2 * r + p) * half, (2 * r + p + 1) * half)
                o_ref[at, lanes] = jnp.where(first_core, pair[p][:half], pair[p][half:])
    m = m_ref[...]
    s = dot(o_ref[...], m)
    for r in range(n_row):
        panel = 2 * jnp.bitwise_xor(row_id, r)
        for p in range(2):
            at = slice((2 * r + p) * half, (2 * r + p + 1) * half)
            keep = keep_ref[1, pl.ds(panel + p, 1)]
            s_ref[at] = jnp.where(keep > 0, s[at], 0.0).astype(jnp.bfloat16)
    res = purify(s_ref[...], m).astype(jnp.bfloat16)
    for r in range(n_row):
        for j in range(n_col // 2):
            lanes = slice(2 * j * blk, (2 * j + 2) * blk)
            upper = res[2 * r * half : (2 * r + 1) * half, lanes]
            lower = res[(2 * r + 1) * half : (2 * r + 2) * half, lanes]
            to = jnp.bitwise_xor(row_id, r) * n_col + 2 * j
            out_ref[to], out_ref[to + 1] = split_pair(upper, lower)


def extra_kernel(plan, keep_ref, *refs):
    row_refs, (out_ref, m_ref, o_ref) = refs[: plan.n_row], refs[plan.n_row :]
    row_id, col_id = lax.axis_index("row"), lax.axis_index("col")
    blk, n_col = plan.blk, plan.n_col
    for k in range(plan.extra):
        at = slice(k * blk, (k + 1) * blk)
        for apart, ref in enumerate(row_refs):
            start = pl.multiple_of(jnp.bitwise_xor(row_id, apart) * 2 * blk, 2 * blk)
            for j in range(n_col // 2):
                lanes = slice(2 * j * blk, (2 * j + 2) * blk)
                low, high = (ref[plan.slot(jnp.bitwise_xor(col_id, 2 * j + c)), at] for c in range(2))
                tile = jnp.concatenate(split_pair(low, high), axis=0)
                m_ref[pl.ds(start, 2 * blk), lanes] = tile
                if apart == 0:
                    o_ref[:, lanes] = tile
        m = m_ref[...]
        s = dot(o_ref[...], m)
        kept = []
        for p in range(2):
            keep = keep_ref[2 + k, pl.ds(2 * row_id + p, 1)]
            kept.append(jnp.where(keep > 0, s[p * blk : (p + 1) * blk], 0.0).astype(jnp.bfloat16))
        res = purify(jnp.concatenate(kept, axis=0), m)
        mine = res[:, : 2 * blk]
        for j in range(1, n_col // 2):
            mine = jnp.where(col_id // 2 == j, res[:, 2 * j * blk : (2 * j + 2) * blk], mine)
        first, second = split_pair(mine[:blk], mine[blk:])
        out_ref[at] = jnp.where(col_id % 2 == 0, first, second).astype(jnp.bfloat16)


def unpack_kernel(plan, kept_hbm, shift_hbm, starts_hbm, ret_ref, *refs):
    *extra_refs, out_hbm, rows_ref, shift_ref, starts_ref, stage, out_ref, sems = refs
    row_id, col_id = lax.axis_index("row"), lax.axis_index("col")
    blk, half, total = plan.blk, plan.half, plan.ndev * plan.rows
    copies = [
        pltpu.make_async_copy(shift_hbm, shift_ref, sems.at[0]),
        pltpu.make_async_copy(kept_hbm.at[pl.ds(2 * row_id, 2)], rows_ref, sems.at[1]),
        pltpu.make_async_copy(starts_hbm, starts_ref, sems.at[2]),
    ]
    for copy in copies:
        copy.start()
    stage[:total] = ret_ref[...]
    for ref in extra_refs:
        stage[total:] = ref[...]
    for copy in copies:
        copy.wait()
    copies = [pltpu.make_async_copy(out_ref.at[p], out_hbm.at[p], sems.at[3 + p]) for p in range(2)]
    for p in range(2):
        base = PANEL - 1 - shift_ref[2 * row_id + p]
        lanes = slice(p * blk, (p + 1) * blk)
        for e in range(rows_ref.shape[2]):
            at = rows_ref[p, col_id, e] + base
            for h in range(2):
                tile = stage[pl.ds(pl.multiple_of(starts_ref[h, at], half), half), :]
                out_ref[p, h * half : (h + 1) * half, e * blk : (e + 1) * blk] = tile[:, lanes].astype(jnp.float32)
        copies[p].start()
    for copy in copies:
        copy.wait()


def swapped(shard, axis, by):
    return lax.ppermute(shard, axis, [(i, i ^ by) for i in range(lax.axis_size(axis))])


def body(density, density_rows, square_rows, panel_shift):
    both = ("row", "col")
    n_row, n_col = lax.axis_size("row"), lax.axis_size("col")
    blk, rh = density.shape[1], density_rows.shape[2]
    npan = density_rows.shape[0]
    plan = Plan(n_row, n_col, blk)
    ndev, rows = plan.ndev, plan.rows
    bf16 = jnp.bfloat16
    size = n_col * blk
    square = pltpu.VMEM((size, size), bf16)
    tables = [pltpu.SMEM((2, npan, rh), jnp.int32), pltpu.SMEM((npan,), jnp.int32)]
    starts = jnp.asarray(plan.starts())

    def blocks(*shape):
        return jax.ShapeDtypeStruct((*shape, 2 * blk), bf16)

    shapes = [blocks(ndev, blk)] + ([blocks(plan.slots, blk)] * plan.line if plan.shared else [])
    packed, *line = pl.pallas_call(
        functools.partial(pack_kernel, plan),
        out_shape=shapes,
        in_specs=[HBM] * 3,
        out_specs=[HBM] * len(shapes),
        scratch_shapes=[pltpu.VMEM(density.shape, bf16)]
        + tables
        + [
            pltpu.VMEM((ndev + plan.line * plan.slots, blk, 2 * blk), bf16),
            pltpu.SemaphoreType.DMA((max(4, len(shapes)),)),
        ],
        compiler_params=PACK_PARAMS,
        name="pack",
    )(density, density_rows, panel_shift)
    y = lax.all_to_all(packed, both, 0, 0, tiled=True)
    sets = 1 + (1 if plan.shared else 0) + plan.extra
    keep = pl.pallas_call(
        functools.partial(mask_kernel, plan),
        out_shape=jax.ShapeDtypeStruct((sets, npan, size), jnp.float32),
        in_specs=[SMEM, VMEM],
        out_specs=VMEM,
        compiler_params=PARAMS,
        name="masks",
    )(panel_shift, square_rows)
    shared, extra = [], []
    if plan.shared:
        line = line[:1] + [swapped(sent, "col", 2 * i) for i, sent in enumerate(line) if i]
        plane = pl.pallas_call(
            functools.partial(regroup_kernel, plan),
            out_shape=[blocks(plan.line, blk)] * n_row + [blocks(plan.line * plan.extra, blk)] * min(1, plan.extra),
            in_specs=[VMEM] * plan.line,
            out_specs=[VMEM] * (n_row + min(1, plan.extra)),
            compiler_params=PARAMS,
            cost_estimate=pl.CostEstimate(flops=20_000_000_000, bytes_accessed=0, transcendentals=0),
            name="regroup",
        )(*line)
        plane, line = plane[:n_row], plane[n_row:]
        own = jnp.concatenate([plane[0]] + [swapped(sent, "row", r) for r, sent in enumerate(plane) if r])
        far = swapped(own, "col", 1)
        shared = pl.pallas_call(
            functools.partial(shared_kernel, plan),
            out_shape=blocks(ndev, plan.half),
            in_specs=[VMEM] * 3,
            out_specs=VMEM,
            scratch_shapes=[square] + [pltpu.VMEM((size // 2, size), bf16)] * 2,
            compiler_params=PARAMS,
            name="shared",
        )(keep, own, far)
        y, keep, shared, *line = lax.optimization_barrier((y, keep, shared, *line))
        shared = [shared]
    if plan.extra:
        line = jnp.concatenate([line[0], swapped(line[0], "col", 1)])
        plane = [line] + [swapped(line, "row", r) for r in range(1, n_row)]
        extra = [
            pl.pallas_call(
                functools.partial(extra_kernel, plan),
                out_shape=blocks(plan.extra * blk),
                in_specs=[VMEM] * (1 + n_row),
                out_specs=VMEM,
                scratch_shapes=[square, pltpu.VMEM((2 * blk, size), bf16)],
                compiler_params=PARAMS,
                name="extra",
            )(keep, *plane)
        ]
    out = pl.pallas_call(
        functools.partial(full_kernel, plan),
        out_shape=blocks(ndev, rows),
        in_specs=[VMEM] * (2 + len(shared)),
        out_specs=HBM,
        scratch_shapes=[square] * 2 + [pltpu.VMEM((ndev, blk, 2 * blk), bf16), pltpu.SemaphoreType.DMA((2,))],
        compiler_params=PARAMS,
        cost_estimate=pl.CostEstimate(flops=4 * size**3, bytes_accessed=4 * ndev * rows * 2 * blk, transcendentals=0),
        name="full",
    )(keep, y, *shared)
    ret = lax.all_to_all(out, both, 0, 0, tiled=True)
    stage = pltpu.VMEM((ndev * rows + plan.extra * blk, 2 * blk), bf16)
    return pl.pallas_call(
        functools.partial(unpack_kernel, plan),
        out_shape=jax.ShapeDtypeStruct(density.shape, jnp.float32),
        in_specs=[HBM] * 3 + [VMEM] * (1 + len(extra)),
        out_specs=HBM,
        scratch_shapes=tables
        + [
            pltpu.SMEM(starts.shape, jnp.int32),
            stage,
            pltpu.VMEM(density.shape, jnp.float32),
            pltpu.SemaphoreType.DMA((5,)),
        ],
        compiler_params=PARAMS,
        name="unpack",
    )(square_rows, panel_shift, starts, ret.reshape(ndev * rows, 2 * blk), *extra)


def solution(mesh):
    placed = (P("row", None, "col"), P(), P(), P())
    return jax.shard_map(
        body, mesh=mesh, in_specs=placed, out_specs=P("row", None, "col"), check_vma=False
    )
```

```python
import functools

import jax
import jax.numpy as jnp
from jax import lax
from jax.experimental import pallas as pl
from jax.experimental.pallas import tpu as pltpu
from jax.sharding import PartitionSpec as P

PANEL = 49

SMEM = pl.BlockSpec(memory_space=pltpu.SMEM)
VMEM = pl.BlockSpec(memory_space=pltpu.VMEM)
HBM = pl.BlockSpec(memory_space=pltpu.HBM)
PARAMS = pltpu.CompilerParams(vmem_limit_bytes=40 * 1024 * 1024)
HINT = 20_000_000_000
PACK_PARAMS = pltpu.CompilerParams(vmem_limit_bytes=63 * 1024 * 1024)


class Plan:
    def __init__(self, n_row, n_col, blk):
        self.n_row, self.n_col, self.blk = n_row, n_col, blk
        self.ndev = n_row * n_col
        self.line = n_col // 2
        chips = self.ndev // 2
        self.full = min(self.ndev, PANEL)
        self.shared = min(chips, PANEL - self.full)
        self.extra = PANEL - self.full - self.shared
        self.slots = self.n_row + self.extra if self.shared else 0

    def residue(self, at):
        return jnp.where(at < PANEL - 1, at + 1, at + 1 - PANEL)

    def send_slot(self, at, chip):
        u = self.residue(at)
        if not self.shared:
            return u
        apart = jnp.bitwise_xor(u - self.full, chip)
        shift = self.line.bit_length() - 1
        plane, line = jnp.right_shift(apart, shift), jnp.bitwise_and(apart, self.line - 1)
        beyond = u - self.full - self.shared
        slot = jnp.where(beyond < 0, line * self.slots + plane, self.n_row + beyond)
        return jnp.where(u < self.full, u, self.ndev + slot)

    def back_slot(self, at, chip):
        u = self.residue(at)
        if not self.shared:
            return u
        apart = jnp.bitwise_xor(u - self.full, chip)
        return self.ndev - self.full + jnp.where(
            jnp.logical_and(u >= self.full, u < self.full + self.shared), self.full + apart, u
        )


def kept_lanes(rows, u, shift, blk):
    npan = rows.shape[0]
    target = u + shift
    target = jnp.where(target >= PANEL, target - PANEL, target)
    has = jnp.sum((rows == target).astype(jnp.float32), axis=1, keepdims=True)
    lane = lax.broadcasted_iota(jnp.int32, (npan, npan * blk), 1)
    tile = lax.broadcasted_iota(jnp.int32, (npan, npan * blk), 0)
    return jnp.sum(jnp.where(lane // blk == tile, has, 0.0), axis=0, keepdims=True)


def pack_kernel(plan, x_hbm, rows_hbm, shift_hbm, *refs):
    *out_refs, x_ref, rows_ref, shift_ref, stage, sems = refs
    row_id, col_id = lax.axis_index("row"), lax.axis_index("col")
    blk, ndev, slots = plan.blk, plan.ndev, plan.slots
    chip = row_id * plan.line + col_id // 2
    copies = [
        pltpu.make_async_copy(shift_hbm, shift_ref, sems.at[0]),
        pltpu.make_async_copy(rows_hbm.at[pl.ds(2 * row_id, 2)], rows_ref, sems.at[1]),
        pltpu.make_async_copy(x_hbm.at[0], x_ref.at[0], sems.at[2]),
        pltpu.make_async_copy(x_hbm.at[1], x_ref.at[1], sems.at[3]),
    ]
    for copy in copies:
        copy.start()
    stage[...] = jnp.zeros_like(stage)
    for copy in copies[:2]:
        copy.wait()
    for p in range(2):
        copies[2 + p].wait()
        base = PANEL - 1 - shift_ref[2 * row_id + p]
        lanes = slice(p * blk, (p + 1) * blk)
        for e in range(rows_ref.shape[2]):
            slot = plan.send_slot(rows_ref[p, col_id, e] + base, chip)
            stage[slot, :, lanes] = x_ref[p, :, e * blk : (e + 1) * blk]
    for k in range(plan.extra):
        block = stage[ndev + plan.n_row + k]
        for i in range(1, plan.line):
            stage[ndev + i * slots + plan.n_row + k] = block
    spans = [(0, ndev)] + [(ndev + i * slots, slots) for i in range(len(out_refs) - 1)]
    copies = [
        pltpu.make_async_copy(stage.at[pl.ds(first, size)], ref, sems.at[i])
        for i, ((first, size), ref) in enumerate(zip(spans, out_refs))
    ]
    for copy in copies:
        copy.start()
    for copy in copies:
        copy.wait()


def mask_kernel(plan, shift_ref, kept_ref, keep_ref):
    me = lax.axis_index("row") * plan.n_col + lax.axis_index("col")
    sets = [jnp.minimum(me, plan.full - 1), plan.full + me // 2]
    sets += [plan.full + plan.shared + k for k in range(plan.extra)]
    for k, u in enumerate(sets[: keep_ref.shape[0]]):
        for panel in range(2 * plan.n_row):
            keep_ref[k, panel : panel + 1] = kept_lanes(kept_ref[panel], u, shift_ref[panel], plan.blk)


def split_pair(low, high):
    blk = low.shape[1] // 2
    first = jnp.concatenate([low[:, :blk], high[:, :blk]], axis=1)
    second = jnp.concatenate([low[:, blk:], high[:, blk:]], axis=1)
    return first, second


def dot(a, b):
    return jnp.dot(a, b, preferred_element_type=jnp.float32)


def purify(s, m):
    return 3.0 * s.astype(jnp.float32) - 2.0 * dot(s, m)


def mask_square(plan, s, keep_ref, k, s_ref):
    for panel in range(2 * plan.n_row):
        at = slice(panel * plan.blk, (panel + 1) * plan.blk)
        s_ref[at] = jnp.where(keep_ref[k, panel : panel + 1] > 0, s[at], 0.0).astype(jnp.bfloat16)


def full_kernel(plan, keep_ref, y_ref, out_hbm, m_ref, s_ref, res_ref, sems):
    blk, n_col = plan.blk, plan.n_col
    for r in range(plan.n_row):
        for j in range(n_col // 2):
            src = r * n_col + 2 * j
            first, second = split_pair(y_ref[src], y_ref[src + 1])
            lanes = slice(2 * j * blk, (2 * j + 2) * blk)
            m_ref[2 * r * blk : (2 * r + 1) * blk, lanes] = first
            m_ref[(2 * r + 1) * blk : (2 * r + 2) * blk, lanes] = second
    m = m_ref[...]
    mask_square(plan, dot(m, m), keep_ref, 0, s_ref)
    copies = []
    for r in range(plan.n_row):
        res = purify(s_ref[2 * r * blk : (2 * r + 2) * blk], m).astype(jnp.bfloat16)
        for j in range(n_col // 2):
            lanes = slice(2 * j * blk, (2 * j + 2) * blk)
            to = r * n_col + 2 * j
            res_ref[to], res_ref[to + 1] = split_pair(res[:blk, lanes], res[blk:, lanes])
        at = pl.ds(r * n_col, n_col)
        copies.append(pltpu.make_async_copy(res_ref.at[at], out_hbm.at[at], sems.at[r]))
        copies[-1].start()
    for copy in copies:
        copy.wait()


def regroup_kernel(plan, *refs):
    line, plane, extra = refs[: plan.line], refs[plan.line : plan.line + plan.n_row], refs[plan.line + plan.n_row :]
    for i, sent in enumerate(line):
        for r, ref in enumerate(plane):
            ref[i] = sent[r]
        for ref in extra:
            for k in range(plan.extra):
                ref[k * plan.line + i] = sent[plan.n_row + k]


def return_kernel(plan, *refs):
    ins, outs = refs[: len(refs) // 2], refs[len(refs) // 2 :]
    for i in range(plan.line):
        for r in range(plan.n_row):
            outs[r][i] = ins[i][r]
    for ref, to in zip(ins[plan.line :], outs[plan.n_row :]):
        to[...] = ref[...]


def shared_kernel(plan, keep_ref, own_ref, far_ref, *refs):
    *out_refs, m_ref, s_ref, res_ref = refs
    n_row, n_col, blk = plan.n_row, plan.n_col, plan.blk
    row_id, col_id = lax.axis_index("row"), lax.axis_index("col")
    first_core = col_id % 2 == 0
    for r in range(n_row):
        start = pl.multiple_of(jnp.bitwise_xor(row_id, r) * 2 * blk, 2 * blk)
        for j in range(plan.line):
            lanes = slice(2 * j * blk, (2 * j + 2) * blk)
            at = r * plan.line + jnp.bitwise_xor(col_id // 2, j)
            own, far = own_ref[at], far_ref[at]
            pair = split_pair(jnp.where(first_core, own, far), jnp.where(first_core, far, own))
            m_ref[pl.ds(start, 2 * blk), lanes] = jnp.concatenate(pair, axis=0)
    m = m_ref[...]
    mask_square(plan, dot(m, m), keep_ref, 1, s_ref)
    res = purify(s_ref[...], m).astype(jnp.bfloat16)
    for row in range(n_row):
        upper, lower = res[2 * row * blk : (2 * row + 1) * blk], res[(2 * row + 1) * blk : (2 * row + 2) * blk]
        for j in range(plan.line):
            lanes = slice(2 * j * blk, (2 * j + 2) * blk)
            first, second = split_pair(upper[:, lanes], lower[:, lanes])
            to = jnp.bitwise_xor(col_id // 2, j) * n_row + jnp.bitwise_xor(row_id, row)
            res_ref[to] = jnp.where(first_core, first, second)
    for i, ref in enumerate(out_refs):
        ref[...] = res_ref[i * n_row : (i + 1) * n_row]


def extra_kernel(plan, keep_ref, far_ref, *refs):
    own_refs, (out_ref, m_ref, o_ref) = refs[: plan.n_row], refs[plan.n_row :]
    row_id, col_id = lax.axis_index("row"), lax.axis_index("col")
    first_core = col_id % 2 == 0
    blk, line = plan.blk, plan.line
    for k in range(plan.extra):
        for r, own_ref in enumerate(own_refs):
            start = pl.multiple_of(jnp.bitwise_xor(row_id, r) * 2 * blk, 2 * blk)
            for j in range(line):
                lanes = slice(2 * j * blk, (2 * j + 2) * blk)
                at = k * line + jnp.bitwise_xor(col_id // 2, j)
                own, far = own_ref[at], far_ref[r * plan.extra * line + at]
                pair = split_pair(jnp.where(first_core, own, far), jnp.where(first_core, far, own))
                tile = jnp.concatenate(pair, axis=0)
                m_ref[pl.ds(start, 2 * blk), lanes] = tile
                if r == 0:
                    o_ref[:, lanes] = tile
        m = m_ref[...]
        s = dot(o_ref[...], m)
        kept = []
        for p in range(2):
            keep = keep_ref[2 + k, pl.ds(2 * row_id + p, 1)]
            kept.append(jnp.where(keep > 0, s[p * blk : (p + 1) * blk], 0.0).astype(jnp.bfloat16))
        res = purify(jnp.concatenate(kept, axis=0), m)
        mine = res[:, : 2 * blk]
        for j in range(1, line):
            mine = jnp.where(col_id // 2 == j, res[:, 2 * j * blk : (2 * j + 2) * blk], mine)
        first, second = split_pair(mine[:blk], mine[blk:])
        out_ref[k] = jnp.where(first_core, first, second).astype(jnp.bfloat16)


def unpack_kernel(plan, kept_hbm, shift_hbm, *refs):
    *in_refs, out_hbm, rows_ref, shift_ref, stage, out_ref, sems = refs
    row_id, col_id = lax.axis_index("row"), lax.axis_index("col")
    blk = plan.blk
    chip = row_id * plan.line + col_id // 2
    copies = [
        pltpu.make_async_copy(shift_hbm, shift_ref, sems.at[0]),
        pltpu.make_async_copy(kept_hbm.at[pl.ds(2 * row_id, 2)], rows_ref, sems.at[1]),
    ]
    for copy in copies:
        copy.start()
    first = 0
    for size, ref in zip([plan.ndev] + [plan.line] * (plan.shared // plan.line) + [plan.extra], in_refs):
        stage[first : first + size] = ref[:size]
        first += size
    for copy in copies:
        copy.wait()
    part = rows_ref.shape[2] // 4
    copies = []
    for p in range(2):
        base = PANEL - 1 - shift_ref[2 * row_id + p]
        lanes = slice(p * blk, (p + 1) * blk)
        for e in range(rows_ref.shape[2]):
            tile = stage[plan.back_slot(rows_ref[p, col_id, e] + base, chip)]
            out_ref[p, :, e * blk : (e + 1) * blk] = tile[:, lanes].astype(jnp.float32)
            if e % part == part - 1:
                at = (p, slice(None), pl.ds((e + 1 - part) * blk, part * blk))
                copies.append(pltpu.make_async_copy(out_ref.at[at], out_hbm.at[at], sems.at[2 + len(copies)]))
                copies[-1].start()
    for copy in copies:
        copy.wait()


def swapped(shard, axis, by):
    return lax.ppermute(shard, axis, [(i, i ^ by) for i in range(lax.axis_size(axis))])


def body(density, density_rows, square_rows, panel_shift):
    both = ("row", "col")
    n_row, n_col = lax.axis_size("row"), lax.axis_size("col")
    blk, rh = density.shape[1], density_rows.shape[2]
    npan = density_rows.shape[0]
    plan = Plan(n_row, n_col, blk)
    ndev = plan.ndev
    bf16 = jnp.bfloat16
    size = n_col * blk
    square = pltpu.VMEM((size, size), bf16)
    tables = [pltpu.SMEM((2, npan, rh), jnp.int32), pltpu.SMEM((npan,), jnp.int32)]

    def blocks(*shape):
        return jax.ShapeDtypeStruct((*shape, 2 * blk), bf16)

    shapes = [blocks(ndev, blk)] + ([blocks(plan.slots, blk)] * plan.line if plan.shared else [])
    packed, *line = pl.pallas_call(
        functools.partial(pack_kernel, plan),
        out_shape=shapes,
        in_specs=[HBM] * 3,
        out_specs=[HBM] * len(shapes),
        scratch_shapes=[pltpu.VMEM(density.shape, bf16)]
        + tables
        + [
            pltpu.VMEM((ndev + plan.line * plan.slots, blk, 2 * blk), bf16),
            pltpu.SemaphoreType.DMA((max(4, len(shapes)),)),
        ],
        compiler_params=PACK_PARAMS,
        name="pack",
    )(density, density_rows, panel_shift)
    y = lax.all_to_all(packed, both, 0, 0, tiled=True)
    sets = 1 + (1 if plan.shared else 0) + plan.extra
    keep = pl.pallas_call(
        functools.partial(mask_kernel, plan),
        out_shape=jax.ShapeDtypeStruct((sets, npan, size), jnp.float32),
        in_specs=[SMEM, VMEM],
        out_specs=VMEM,
        compiler_params=PARAMS,
        name="masks",
    )(panel_shift, square_rows)
    back, extra = [], []
    if plan.shared:

        def regroup(kernel, shapes, name, *operands):
            return pl.pallas_call(
                functools.partial(kernel, plan),
                out_shape=shapes,
                in_specs=[VMEM] * len(operands),
                out_specs=[VMEM] * len(shapes),
                compiler_params=PARAMS,
                cost_estimate=pl.CostEstimate(flops=HINT, bytes_accessed=0, transcendentals=0),
                name=name,
            )(*operands)

        line = line[:1] + [swapped(sent, "col", 2 * i) for i, sent in enumerate(line) if i]
        shapes = [blocks(plan.line, blk)] * n_row + [blocks(plan.line * plan.extra, blk)] * min(1, plan.extra)
        plane = list(regroup(regroup_kernel, shapes, "regroup", *line))
        plane, rest = plane[:n_row], plane[n_row:]
        own = jnp.concatenate([plane[0]] + [swapped(sent, "row", r) for r, sent in enumerate(plane) if r])
        far = swapped(own, "col", 1)
        back = pl.pallas_call(
            functools.partial(shared_kernel, plan),
            out_shape=[blocks(n_row, blk)] * plan.line,
            in_specs=[VMEM] * 3,
            out_specs=[VMEM] * plan.line,
            scratch_shapes=[square] * 2 + [pltpu.VMEM((plan.shared, blk, 2 * blk), bf16)],
            compiler_params=PARAMS,
            name="shared",
        )(keep, own, far)
        y, keep, first, *rest = lax.optimization_barrier((y, keep, back[0], *rest))
        back = [first] + list(back[1:])
        back = back[:1] + [swapped(sent, "col", 2 * i) for i, sent in enumerate(back) if i]
        back = list(regroup(return_kernel, shapes, "regroup_back", *back, *rest))
        back, rest = back[:n_row], back[n_row:]
        rest = rest + [swapped(sent, "row", r) for sent in rest for r in range(1, n_row)]
        back = [back[0]] + [swapped(sent, "row", r) for r, sent in enumerate(back) if r]
        if plan.extra:
            tied = lax.optimization_barrier((*rest, *back))
            rest, back = tied[:n_row], tied[n_row:]
    if plan.extra:
        far = swapped(jnp.concatenate(rest), "col", 1)
        extra = pl.pallas_call(
            functools.partial(extra_kernel, plan),
            out_shape=blocks(plan.extra, blk),
            in_specs=[VMEM] * (2 + n_row),
            out_specs=VMEM,
            scratch_shapes=[square, pltpu.VMEM((2 * blk, size), bf16)],
            compiler_params=PARAMS,
            name="extra",
        )(keep, far, *rest)
        extra = [extra]
    out = pl.pallas_call(
        functools.partial(full_kernel, plan),
        out_shape=blocks(ndev, blk),
        in_specs=[VMEM] * 2,
        out_specs=HBM,
        scratch_shapes=[square] * 2 + [pltpu.VMEM((ndev, blk, 2 * blk), bf16), pltpu.SemaphoreType.DMA((n_row,))],
        compiler_params=PARAMS,
        cost_estimate=pl.CostEstimate(flops=4 * size**3, bytes_accessed=8 * ndev * blk * blk, transcendentals=0),
        name="full",
    )(keep, y)
    ret = lax.all_to_all(out, both, 0, 0, tiled=True)
    return pl.pallas_call(
        functools.partial(unpack_kernel, plan),
        out_shape=jax.ShapeDtypeStruct(density.shape, jnp.float32),
        in_specs=[HBM] * 2 + [VMEM] * (1 + len(back) + len(extra)),
        out_specs=HBM,
        scratch_shapes=tables
        + [
            pltpu.VMEM((ndev + plan.shared + plan.extra, blk, 2 * blk), bf16),
            pltpu.VMEM(density.shape, jnp.float32),
            pltpu.SemaphoreType.DMA((10,)),
        ],
        compiler_params=PARAMS,
        name="unpack",
    )(square_rows, panel_shift, ret, *back, *extra)


def solution(mesh):
    placed = (P("row", None, "col"), P(), P(), P())
    return jax.shard_map(
        body, mesh=mesh, in_specs=placed, out_specs=P("row", None, "col"), check_vma=False
    )
```

```python
import functools

import jax
import jax.numpy as jnp
from jax import lax
from jax.experimental import pallas as pl
from jax.experimental.pallas import tpu as pltpu
from jax.sharding import PartitionSpec as P

PANEL = 49

SMEM = pl.BlockSpec(memory_space=pltpu.SMEM)
VMEM = pl.BlockSpec(memory_space=pltpu.VMEM)
HBM = pl.BlockSpec(memory_space=pltpu.HBM)
PARAMS = pltpu.CompilerParams(vmem_limit_bytes=40 * 1024 * 1024)
HINT = 20_000_000_000
PACK_PARAMS = pltpu.CompilerParams(vmem_limit_bytes=63 * 1024 * 1024)


class Plan:
    def __init__(self, n_row, n_col, blk):
        self.n_row, self.n_col, self.blk = n_row, n_col, blk
        self.ndev = n_row * n_col
        self.line = n_col // 2
        chips = self.ndev // 2
        self.full = min(self.ndev, PANEL)
        self.shared = min(chips, PANEL - self.full)
        self.extra = PANEL - self.full - self.shared
        self.slots = self.n_row + self.extra if self.shared else 0

    def residue(self, at):
        return jnp.where(at < PANEL - 1, at + 1, at + 1 - PANEL)

    def send_slot(self, at, chip):
        u = self.residue(at)
        if not self.shared:
            return u
        apart = jnp.bitwise_xor(u - self.full, chip)
        shift = self.line.bit_length() - 1
        plane, line = jnp.right_shift(apart, shift), jnp.bitwise_and(apart, self.line - 1)
        beyond = u - self.full - self.shared
        slot = jnp.where(beyond < 0, line * self.slots + plane, self.n_row + beyond)
        return jnp.where(u < self.full, u, self.ndev + slot)

    def back_slot(self, at, chip):
        u = self.residue(at)
        if not self.shared:
            return u
        apart = jnp.bitwise_xor(u - self.full, chip)
        return self.ndev - self.full + jnp.where(
            jnp.logical_and(u >= self.full, u < self.full + self.shared), self.full + apart, u
        )


def kept_lanes(rows, u, shift, blk):
    npan = rows.shape[0]
    target = u + shift
    target = jnp.where(target >= PANEL, target - PANEL, target)
    has = jnp.sum((rows == target).astype(jnp.float32), axis=1, keepdims=True)
    lane = lax.broadcasted_iota(jnp.int32, (npan, npan * blk), 1)
    tile = lax.broadcasted_iota(jnp.int32, (npan, npan * blk), 0)
    return jnp.sum(jnp.where(lane // blk == tile, has, 0.0), axis=0, keepdims=True)


def pack_kernel(plan, x_hbm, rows_hbm, shift_hbm, *refs):
    *out_refs, x_ref, rows_ref, shift_ref, stage, sems = refs
    row_id, col_id = lax.axis_index("row"), lax.axis_index("col")
    blk, ndev, slots = plan.blk, plan.ndev, plan.slots
    chip = row_id * plan.line + col_id // 2
    copies = [
        pltpu.make_async_copy(shift_hbm, shift_ref, sems.at[0]),
        pltpu.make_async_copy(rows_hbm.at[pl.ds(2 * row_id, 2)], rows_ref, sems.at[1]),
        pltpu.make_async_copy(x_hbm.at[0], x_ref.at[0], sems.at[2]),
        pltpu.make_async_copy(x_hbm.at[1], x_ref.at[1], sems.at[3]),
    ]
    for copy in copies:
        copy.start()
    stage[...] = jnp.zeros_like(stage)
    for copy in copies[:2]:
        copy.wait()
    for p in range(2):
        copies[2 + p].wait()
        base = PANEL - 1 - shift_ref[2 * row_id + p]
        lanes = slice(p * blk, (p + 1) * blk)
        for e in range(rows_ref.shape[2]):
            slot = plan.send_slot(rows_ref[p, col_id, e] + base, chip)
            stage[slot, :, lanes] = x_ref[p, :, e * blk : (e + 1) * blk]
    for k in range(plan.extra):
        block = stage[ndev + plan.n_row + k]
        for i in range(1, plan.line):
            stage[ndev + i * slots + plan.n_row + k] = block
    spans = [(0, ndev)] + [(ndev + i * slots, slots) for i in range(len(out_refs) - 1)]
    copies = [
        pltpu.make_async_copy(stage.at[pl.ds(first, size)], ref, sems.at[i])
        for i, ((first, size), ref) in enumerate(zip(spans, out_refs))
    ]
    for copy in copies:
        copy.start()
    for copy in copies:
        copy.wait()


def mask_kernel(plan, shift_ref, kept_ref, keep_ref):
    me = lax.axis_index("row") * plan.n_col + lax.axis_index("col")
    sets = [jnp.minimum(me, plan.full - 1), plan.full + me // 2]
    sets += [plan.full + plan.shared + k for k in range(plan.extra)]
    for k, u in enumerate(sets[: keep_ref.shape[0]]):
        for panel in range(2 * plan.n_row):
            keep_ref[k, panel : panel + 1] = kept_lanes(kept_ref[panel], u, shift_ref[panel], plan.blk)


def split_pair(low, high):
    blk = low.shape[1] // 2
    first = jnp.concatenate([low[:, :blk], high[:, :blk]], axis=1)
    second = jnp.concatenate([low[:, blk:], high[:, blk:]], axis=1)
    return first, second


def dot(a, b):
    return jnp.dot(a, b, preferred_element_type=jnp.float32)


def purify(s, m):
    return 3.0 * s.astype(jnp.float32) - 2.0 * dot(s, m)


def mask_square(plan, s, keep_ref, k, s_ref):
    for panel in range(2 * plan.n_row):
        at = slice(panel * plan.blk, (panel + 1) * plan.blk)
        s_ref[at] = jnp.where(keep_ref[k, panel : panel + 1] > 0, s[at], 0.0).astype(jnp.bfloat16)


def full_kernel(plan, keep_ref, y_ref, out_hbm, m_ref, s_ref, res_ref, sems):
    blk, n_col = plan.blk, plan.n_col
    for r in range(plan.n_row):
        for j in range(n_col // 2):
            src = r * n_col + 2 * j
            first, second = split_pair(y_ref[src], y_ref[src + 1])
            lanes = slice(2 * j * blk, (2 * j + 2) * blk)
            m_ref[2 * r * blk : (2 * r + 1) * blk, lanes] = first
            m_ref[(2 * r + 1) * blk : (2 * r + 2) * blk, lanes] = second
    m = m_ref[...]
    mask_square(plan, dot(m, m), keep_ref, 0, s_ref)
    copies = []
    for r in range(plan.n_row):
        res = purify(s_ref[2 * r * blk : (2 * r + 2) * blk], m).astype(jnp.bfloat16)
        for j in range(n_col // 2):
            lanes = slice(2 * j * blk, (2 * j + 2) * blk)
            to = r * n_col + 2 * j
            res_ref[to], res_ref[to + 1] = split_pair(res[:blk, lanes], res[blk:, lanes])
        at = pl.ds(r * n_col, n_col)
        copies.append(pltpu.make_async_copy(res_ref.at[at], out_hbm.at[at], sems.at[r]))
        copies[-1].start()
    for copy in copies:
        copy.wait()


def regroup_kernel(plan, *refs):
    line, plane, extra = refs[: plan.line], refs[plan.line : plan.line + plan.n_row], refs[plan.line + plan.n_row :]
    for i, sent in enumerate(line):
        for r, ref in enumerate(plane):
            ref[i] = sent[r]
        for ref in extra:
            for k in range(plan.extra):
                ref[k * plan.line + i] = sent[plan.n_row + k]


def return_kernel(plan, *refs):
    passed = (len(refs) - 2 - plan.n_row) // 2
    ins, outs = refs[: 2 + passed], refs[2 + passed :]
    half = plan.line // 2
    for r in range(plan.n_row):
        for s in range(2):
            for i in range(half):
                outs[r][s * half + i] = ins[s][i * plan.n_row + r]
    for ref, to in zip(ins[2:], outs[plan.n_row :]):
        to[...] = ref[...]


def join_kernel(plan, *refs):
    *parts, out_ref = refs
    first = 0
    for ref in parts:
        out_ref[first : first + ref.shape[0]] = ref[...]
        first += ref.shape[0]


def sort_kernel(plan, *refs):
    plane, outs = refs[: plan.n_row], refs[plan.n_row :]
    for r, sent in enumerate(plane):
        for s in range(2):
            for i, ref in enumerate(outs):
                ref[2 * r + s] = sent[2 * s + i]


def shared_kernel(plan, keep_ref, own_ref, far_ref, *refs):
    *out_refs, m_ref, s_ref, res_ref = refs
    n_row, n_col, blk = plan.n_row, plan.n_col, plan.blk
    row_id, col_id = lax.axis_index("row"), lax.axis_index("col")
    first_core = col_id % 2 == 0
    for r in range(n_row):
        start = pl.multiple_of(jnp.bitwise_xor(row_id, r) * 2 * blk, 2 * blk)
        for j in range(plan.line):
            lanes = slice(2 * j * blk, (2 * j + 2) * blk)
            at = r * plan.line + jnp.bitwise_xor(col_id // 2, j)
            own, far = own_ref[at], far_ref[at]
            pair = split_pair(jnp.where(first_core, own, far), jnp.where(first_core, far, own))
            m_ref[pl.ds(start, 2 * blk), lanes] = jnp.concatenate(pair, axis=0)
    m = m_ref[...]
    mask_square(plan, dot(m, m), keep_ref, 1, s_ref)
    res = purify(s_ref[...], m).astype(jnp.bfloat16)
    for row in range(n_row):
        upper, lower = res[2 * row * blk : (2 * row + 1) * blk], res[(2 * row + 1) * blk : (2 * row + 2) * blk]
        for j in range(plan.line):
            lanes = slice(2 * j * blk, (2 * j + 2) * blk)
            first, second = split_pair(upper[:, lanes], lower[:, lanes])
            to = jnp.bitwise_xor(col_id // 2, j) * n_row + jnp.bitwise_xor(row_id, row)
            res_ref[to] = jnp.where(first_core, first, second)
    for i, ref in enumerate(out_refs):
        ref[...] = res_ref[i * ref.shape[0] : (i + 1) * ref.shape[0]]


def extra_kernel(plan, keep_ref, far_ref, *refs):
    own_refs, (out_ref, m_ref, o_ref) = refs[: plan.n_row], refs[plan.n_row :]
    row_id, col_id = lax.axis_index("row"), lax.axis_index("col")
    first_core = col_id % 2 == 0
    blk, line = plan.blk, plan.line
    for k in range(plan.extra):
        for r, own_ref in enumerate(own_refs):
            start = pl.multiple_of(jnp.bitwise_xor(row_id, r) * 2 * blk, 2 * blk)
            for j in range(line):
                lanes = slice(2 * j * blk, (2 * j + 2) * blk)
                at = k * line + jnp.bitwise_xor(col_id // 2, j)
                own, far = own_ref[at], far_ref[r * plan.extra * line + at]
                pair = split_pair(jnp.where(first_core, own, far), jnp.where(first_core, far, own))
                tile = jnp.concatenate(pair, axis=0)
                m_ref[pl.ds(start, 2 * blk), lanes] = tile
                if r == 0:
                    o_ref[:, lanes] = tile
        m = m_ref[...]
        s = dot(o_ref[...], m)
        kept = []
        for p in range(2):
            keep = keep_ref[2 + k, pl.ds(2 * row_id + p, 1)]
            kept.append(jnp.where(keep > 0, s[p * blk : (p + 1) * blk], 0.0).astype(jnp.bfloat16))
        res = purify(jnp.concatenate(kept, axis=0), m)
        mine = res[:, : 2 * blk]
        for j in range(1, line):
            mine = jnp.where(col_id // 2 == j, res[:, 2 * j * blk : (2 * j + 2) * blk], mine)
        first, second = split_pair(mine[:blk], mine[blk:])
        out_ref[k] = jnp.where(first_core, first, second).astype(jnp.bfloat16)


def unpack_kernel(plan, kept_hbm, shift_hbm, *refs):
    *in_refs, out_hbm, rows_ref, shift_ref, stage, out_ref, sems = refs
    row_id, col_id = lax.axis_index("row"), lax.axis_index("col")
    blk = plan.blk
    chip = row_id * plan.line + col_id // 2
    copies = [
        pltpu.make_async_copy(shift_hbm, shift_ref, sems.at[0]),
        pltpu.make_async_copy(kept_hbm.at[pl.ds(2 * row_id, 2)], rows_ref, sems.at[1]),
    ]
    for copy in copies:
        copy.start()
    ret_ref, *more_refs = in_refs
    stage[: plan.ndev] = ret_ref[...]
    if plan.shared:
        half = plan.shared // 2
        for k in range(half):
            for i in range(2):
                stage[plan.ndev + 2 * k + i] = more_refs[0][i * half + k]
        for ref in more_refs[1:]:
            stage[plan.ndev + plan.shared :] = ref[...]
    for copy in copies:
        copy.wait()
    part = rows_ref.shape[2] // 4
    copies = []
    for p in range(2):
        base = PANEL - 1 - shift_ref[2 * row_id + p]
        lanes = slice(p * blk, (p + 1) * blk)
        for e in range(rows_ref.shape[2]):
            tile = stage[plan.back_slot(rows_ref[p, col_id, e] + base, chip)]
            out_ref[p, :, e * blk : (e + 1) * blk] = tile[:, lanes].astype(jnp.float32)
            if e % part == part - 1:
                at = (p, slice(None), pl.ds((e + 1 - part) * blk, part * blk))
                copies.append(pltpu.make_async_copy(out_ref.at[at], out_hbm.at[at], sems.at[2 + len(copies)]))
                copies[-1].start()
    for copy in copies:
        copy.wait()


def swapped(shard, axis, by):
    return lax.ppermute(shard, axis, [(i, i ^ by) for i in range(lax.axis_size(axis))])


def body(density, density_rows, square_rows, panel_shift):
    both = ("row", "col")
    n_row, n_col = lax.axis_size("row"), lax.axis_size("col")
    blk, rh = density.shape[1], density_rows.shape[2]
    npan = density_rows.shape[0]
    plan = Plan(n_row, n_col, blk)
    ndev = plan.ndev
    bf16 = jnp.bfloat16
    size = n_col * blk
    square = pltpu.VMEM((size, size), bf16)
    tables = [pltpu.SMEM((2, npan, rh), jnp.int32), pltpu.SMEM((npan,), jnp.int32)]

    def blocks(*shape):
        return jax.ShapeDtypeStruct((*shape, 2 * blk), bf16)

    shapes = [blocks(ndev, blk)] + ([blocks(plan.slots, blk)] * plan.line if plan.shared else [])
    packed, *line = pl.pallas_call(
        functools.partial(pack_kernel, plan),
        out_shape=shapes,
        in_specs=[HBM] * 3,
        out_specs=[HBM] * len(shapes),
        scratch_shapes=[pltpu.VMEM(density.shape, bf16)]
        + tables
        + [
            pltpu.VMEM((ndev + plan.line * plan.slots, blk, 2 * blk), bf16),
            pltpu.SemaphoreType.DMA((max(4, len(shapes)),)),
        ],
        compiler_params=PACK_PARAMS,
        name="pack",
    )(density, density_rows, panel_shift)
    y = lax.all_to_all(packed, both, 0, 0, tiled=True)
    sets = 1 + (1 if plan.shared else 0) + plan.extra
    keep = pl.pallas_call(
        functools.partial(mask_kernel, plan),
        out_shape=jax.ShapeDtypeStruct((sets, npan, size), jnp.float32),
        in_specs=[SMEM, VMEM],
        out_specs=VMEM,
        compiler_params=PARAMS,
        name="masks",
    )(panel_shift, square_rows)
    back, extra = [], []
    if plan.shared:

        def regroup(kernel, shapes, name, *operands):
            return pl.pallas_call(
                functools.partial(kernel, plan),
                out_shape=shapes,
                in_specs=[VMEM] * len(operands),
                out_specs=[VMEM] * len(shapes),
                compiler_params=PARAMS,
                cost_estimate=pl.CostEstimate(flops=HINT, bytes_accessed=0, transcendentals=0),
                name=name,
            )(*operands)

        line = line[:1] + [swapped(sent, "col", 2 * i) for i, sent in enumerate(line) if i]
        shapes = [blocks(plan.line, blk)] * n_row + [blocks(plan.line * plan.extra, blk)] * min(1, plan.extra)
        plane = list(regroup(regroup_kernel, shapes, "regroup", *line))
        plane, rest = plane[:n_row], plane[n_row:]
        own = jnp.concatenate([plane[0]] + [swapped(sent, "row", r) for r, sent in enumerate(plane) if r])
        far = swapped(own, "col", 1)
        back = pl.pallas_call(
            functools.partial(shared_kernel, plan),
            out_shape=[blocks(plan.shared // 2, blk)] * 2,
            in_specs=[VMEM] * 3,
            out_specs=[VMEM] * 2,
            scratch_shapes=[square] * 2 + [pltpu.VMEM((plan.shared, blk, 2 * blk), bf16)],
            compiler_params=PARAMS,
            name="shared",
        )(keep, own, far)
        y, keep, first, *rest = lax.optimization_barrier((y, keep, back[0], *rest))
        back = [first, swapped(back[1], "col", plan.line)]
        shapes = [blocks(plan.line, blk)] * n_row + [blocks(plan.line * plan.extra, blk)] * min(1, plan.extra)
        back = list(regroup(return_kernel, shapes, "regroup_back", *back, *rest))
        back, rest = back[:n_row], back[n_row:]
        rest = rest + [swapped(sent, "row", r) for sent in rest for r in range(1, n_row)]
        back = [back[0]] + [swapped(sent, "row", r) for r, sent in enumerate(back) if r]
        back = pl.pallas_call(
            functools.partial(sort_kernel, plan),
            out_shape=[blocks(plan.shared // 2, blk)] * 2,
            in_specs=[VMEM] * n_row,
            out_specs=[VMEM] * 2,
            compiler_params=PARAMS,
            cost_estimate=pl.CostEstimate(flops=500_000_000, bytes_accessed=0, transcendentals=0),
            name="sort",
        )(*back)
        back = [back[0], swapped(back[1], "col", 2)]

        def join(hint, name, *parts):
            return pl.pallas_call(
                functools.partial(join_kernel, plan),
                out_shape=blocks(sum(part.shape[0] for part in parts), blk),
                in_specs=[VMEM] * len(parts),
                out_specs=VMEM,
                compiler_params=PARAMS,
                cost_estimate=pl.CostEstimate(flops=hint, bytes_accessed=0, transcendentals=0),
                name=name,
            )(*parts)

        back = [join(4_000_000_000, "join_back", *back)]
    if plan.extra:
        far = swapped(join(1_500_000_000, "join", *rest), "col", 1)
        far, *back = lax.optimization_barrier((far, *back))
        extra = pl.pallas_call(
            functools.partial(extra_kernel, plan),
            out_shape=blocks(plan.extra, blk),
            in_specs=[VMEM] * (2 + n_row),
            out_specs=VMEM,
            scratch_shapes=[square, pltpu.VMEM((2 * blk, size), bf16)],
            compiler_params=PARAMS,
            name="extra",
        )(keep, far, *rest)
        extra = [extra]
    out = pl.pallas_call(
        functools.partial(full_kernel, plan),
        out_shape=blocks(ndev, blk),
        in_specs=[VMEM] * 2,
        out_specs=HBM,
        scratch_shapes=[square] * 2 + [pltpu.VMEM((ndev, blk, 2 * blk), bf16), pltpu.SemaphoreType.DMA((n_row,))],
        compiler_params=PARAMS,
        cost_estimate=pl.CostEstimate(flops=4 * size**3, bytes_accessed=8 * ndev * blk * blk, transcendentals=0),
        name="full",
    )(keep, y)
    ret = lax.all_to_all(out, both, 0, 0, tiled=True)
    return pl.pallas_call(
        functools.partial(unpack_kernel, plan),
        out_shape=jax.ShapeDtypeStruct(density.shape, jnp.float32),
        in_specs=[HBM] * 2 + [VMEM] * (1 + len(back) + len(extra)),
        out_specs=HBM,
        scratch_shapes=tables
        + [
            pltpu.VMEM((ndev + plan.shared + plan.extra, blk, 2 * blk), bf16),
            pltpu.VMEM(density.shape, jnp.float32),
            pltpu.SemaphoreType.DMA((10,)),
        ],
        compiler_params=PARAMS,
        name="unpack",
    )(square_rows, panel_shift, ret, *back, *extra)


def solution(mesh):
    placed = (P("row", None, "col"), P(), P(), P())
    return jax.shard_map(
        body, mesh=mesh, in_specs=placed, out_specs=P("row", None, "col"), check_vma=False
    )
```

```python
import functools

import jax
import jax.numpy as jnp
from jax import lax
from jax.experimental import pallas as pl
from jax.experimental.pallas import tpu as pltpu
from jax.sharding import PartitionSpec as P

PANEL = 49

SMEM = pl.BlockSpec(memory_space=pltpu.SMEM)
VMEM = pl.BlockSpec(memory_space=pltpu.VMEM)
HBM = pl.BlockSpec(memory_space=pltpu.HBM)
PARAMS = pltpu.CompilerParams(vmem_limit_bytes=40 * 1024 * 1024)
HINT = 20_000_000_000
PACK_PARAMS = pltpu.CompilerParams(vmem_limit_bytes=63 * 1024 * 1024)


class Plan:
    def __init__(self, n_row, n_col, blk):
        self.n_row, self.n_col, self.blk = n_row, n_col, blk
        self.ndev = n_row * n_col
        self.line = n_col // 2
        chips = self.ndev // 2
        self.full = min(self.ndev, PANEL)
        self.shared = min(chips, PANEL - self.full)
        self.extra = PANEL - self.full - self.shared
        self.slots = self.n_row + self.extra if self.shared else 0

    def residue(self, at):
        return jnp.where(at < PANEL - 1, at + 1, at + 1 - PANEL)

    def send_slot(self, at, chip):
        u = self.residue(at)
        if not self.shared:
            return u
        apart = jnp.bitwise_xor(u - self.full, chip)
        shift = self.line.bit_length() - 1
        plane, line = jnp.right_shift(apart, shift), jnp.bitwise_and(apart, self.line - 1)
        beyond = u - self.full - self.shared
        slot = jnp.where(beyond < 0, line * self.slots + plane, self.n_row + beyond)
        return jnp.where(u < self.full, u, self.ndev + slot)

    def back_slot(self, at, chip):
        u = self.residue(at)
        if not self.shared:
            return u
        apart = jnp.bitwise_xor(u - self.full, chip)
        return self.ndev - self.full + jnp.where(
            jnp.logical_and(u >= self.full, u < self.full + self.shared), self.full + apart, u
        )


def kept_lanes(rows, u, shift, blk):
    npan = rows.shape[0]
    target = u + shift
    target = jnp.where(target >= PANEL, target - PANEL, target)
    has = jnp.sum((rows == target).astype(jnp.float32), axis=1, keepdims=True)
    lane = lax.broadcasted_iota(jnp.int32, (npan, npan * blk), 1)
    tile = lax.broadcasted_iota(jnp.int32, (npan, npan * blk), 0)
    return jnp.sum(jnp.where(lane // blk == tile, has, 0.0), axis=0, keepdims=True)


def pack_kernel(plan, x_hbm, rows_hbm, shift_hbm, *refs):
    *out_refs, x_ref, rows_ref, shift_ref, stage, sems = refs
    row_id, col_id = lax.axis_index("row"), lax.axis_index("col")
    blk, ndev, slots = plan.blk, plan.ndev, plan.slots
    chip = row_id * plan.line + col_id // 2
    copies = [
        pltpu.make_async_copy(shift_hbm, shift_ref, sems.at[0]),
        pltpu.make_async_copy(rows_hbm.at[pl.ds(2 * row_id, 2)], rows_ref, sems.at[1]),
        pltpu.make_async_copy(x_hbm.at[0], x_ref.at[0], sems.at[2]),
        pltpu.make_async_copy(x_hbm.at[1], x_ref.at[1], sems.at[3]),
    ]
    for copy in copies:
        copy.start()
    stage[...] = jnp.zeros_like(stage)
    for copy in copies[:2]:
        copy.wait()
    for p in range(2):
        copies[2 + p].wait()
        base = PANEL - 1 - shift_ref[2 * row_id + p]
        lanes = slice(p * blk, (p + 1) * blk)
        for e in range(rows_ref.shape[2]):
            slot = plan.send_slot(rows_ref[p, col_id, e] + base, chip)
            stage[slot, :, lanes] = x_ref[p, :, e * blk : (e + 1) * blk]
    for k in range(plan.extra):
        block = stage[ndev + plan.n_row + k]
        for i in range(1, plan.line):
            stage[ndev + i * slots + plan.n_row + k] = block
    spans = [(0, ndev)] + [(ndev + i * slots, slots) for i in range(len(out_refs) - 1)]
    copies = [
        pltpu.make_async_copy(stage.at[pl.ds(first, size)], ref, sems.at[i])
        for i, ((first, size), ref) in enumerate(zip(spans, out_refs))
    ]
    for copy in copies:
        copy.start()
    for copy in copies:
        copy.wait()


def mask_kernel(plan, shift_ref, kept_ref, keep_ref):
    me = lax.axis_index("row") * plan.n_col + lax.axis_index("col")
    sets = [jnp.minimum(me, plan.full - 1), plan.full + me // 2]
    sets += [plan.full + plan.shared + k for k in range(plan.extra)]
    for k, u in enumerate(sets[: keep_ref.shape[0]]):
        for panel in range(2 * plan.n_row):
            keep_ref[k, panel : panel + 1] = kept_lanes(kept_ref[panel], u, shift_ref[panel], plan.blk)


def split_pair(low, high):
    blk = low.shape[1] // 2
    first = jnp.concatenate([low[:, :blk], high[:, :blk]], axis=1)
    second = jnp.concatenate([low[:, blk:], high[:, blk:]], axis=1)
    return first, second


def dot(a, b):
    return jnp.dot(a, b, preferred_element_type=jnp.float32)


def purify(s, m):
    return 3.0 * s.astype(jnp.float32) - 2.0 * dot(s, m)


def mask_square(plan, s, keep_ref, k, s_ref):
    for panel in range(2 * plan.n_row):
        at = slice(panel * plan.blk, (panel + 1) * plan.blk)
        s_ref[at] = jnp.where(keep_ref[k, panel : panel + 1] > 0, s[at], 0.0).astype(jnp.bfloat16)


def full_kernel(plan, keep_ref, y_ref, res_ref, m_ref, s_ref):
    blk, n_col = plan.blk, plan.n_col
    for r in range(plan.n_row):
        for j in range(n_col // 2):
            src = r * n_col + 2 * j
            first, second = split_pair(y_ref[src], y_ref[src + 1])
            lanes = slice(2 * j * blk, (2 * j + 2) * blk)
            m_ref[2 * r * blk : (2 * r + 1) * blk, lanes] = first
            m_ref[(2 * r + 1) * blk : (2 * r + 2) * blk, lanes] = second
    m = m_ref[...]
    mask_square(plan, dot(m, m), keep_ref, 0, s_ref)
    for r in range(plan.n_row):
        res = purify(s_ref[2 * r * blk : (2 * r + 2) * blk], m).astype(jnp.bfloat16)
        for j in range(n_col // 2):
            lanes = slice(2 * j * blk, (2 * j + 2) * blk)
            to = r * n_col + 2 * j
            res_ref[to], res_ref[to + 1] = split_pair(res[:blk, lanes], res[blk:, lanes])


def regroup_kernel(plan, *refs):
    line, plane, extra = refs[: plan.line], refs[plan.line : plan.line + plan.n_row], refs[plan.line + plan.n_row :]
    for i, sent in enumerate(line):
        for r, ref in enumerate(plane):
            ref[i] = sent[r]
        for ref in extra:
            for k in range(plan.extra):
                ref[k * plan.line + i] = sent[plan.n_row + k]


def return_kernel(plan, *refs):
    passed = (len(refs) - 2 - plan.n_row) // 2
    ins, outs = refs[: 2 + passed], refs[2 + passed :]
    half = plan.line // 2
    for r in range(plan.n_row):
        for s in range(2):
            for i in range(half):
                outs[r][s * half + i] = ins[s][i * plan.n_row + r]
    for ref, to in zip(ins[2:], outs[plan.n_row :]):
        to[...] = ref[...]


def join_kernel(plan, *refs):
    *parts, out_ref = refs
    first = 0
    for ref in parts:
        out_ref[first : first + ref.shape[0]] = ref[...]
        first += ref.shape[0]


def sort_kernel(plan, *refs):
    plane, outs = refs[: plan.n_row], refs[plan.n_row :]
    for r, sent in enumerate(plane):
        for s in range(2):
            for i, ref in enumerate(outs):
                ref[2 * r + s] = sent[2 * s + i]


def shared_kernel(plan, keep_ref, own_ref, far_ref, *refs):
    *out_refs, m_ref, s_ref, res_ref = refs
    n_row, n_col, blk = plan.n_row, plan.n_col, plan.blk
    row_id, col_id = lax.axis_index("row"), lax.axis_index("col")
    first_core = col_id % 2 == 0
    for r in range(n_row):
        start = pl.multiple_of(jnp.bitwise_xor(row_id, r) * 2 * blk, 2 * blk)
        for j in range(plan.line):
            lanes = slice(2 * j * blk, (2 * j + 2) * blk)
            at = r * plan.line + jnp.bitwise_xor(col_id // 2, j)
            own, far = own_ref[at], far_ref[at]
            pair = split_pair(jnp.where(first_core, own, far), jnp.where(first_core, far, own))
            m_ref[pl.ds(start, 2 * blk), lanes] = jnp.concatenate(pair, axis=0)
    m = m_ref[...]
    mask_square(plan, dot(m, m), keep_ref, 1, s_ref)
    res = purify(s_ref[...], m).astype(jnp.bfloat16)
    for row in range(n_row):
        upper, lower = res[2 * row * blk : (2 * row + 1) * blk], res[(2 * row + 1) * blk : (2 * row + 2) * blk]
        for j in range(plan.line):
            lanes = slice(2 * j * blk, (2 * j + 2) * blk)
            first, second = split_pair(upper[:, lanes], lower[:, lanes])
            to = jnp.bitwise_xor(col_id // 2, j) * n_row + jnp.bitwise_xor(row_id, row)
            res_ref[to] = jnp.where(first_core, first, second)
    for i, ref in enumerate(out_refs):
        ref[...] = res_ref[i * ref.shape[0] : (i + 1) * ref.shape[0]]


def extra_block(plan, k, keep_ref, far_ref, *refs):
    own_refs, (m_ref, o_ref) = refs[: plan.n_row], refs[plan.n_row :]
    row_id, col_id = lax.axis_index("row"), lax.axis_index("col")
    first_core = col_id % 2 == 0
    blk, line = plan.blk, plan.line
    for r, own_ref in enumerate(own_refs):
        start = pl.multiple_of(jnp.bitwise_xor(row_id, r) * 2 * blk, 2 * blk)
        for j in range(line):
            lanes = slice(2 * j * blk, (2 * j + 2) * blk)
            at = k * line + jnp.bitwise_xor(col_id // 2, j)
            own, far = own_ref[at], far_ref[r * plan.extra * line + at]
            pair = split_pair(jnp.where(first_core, own, far), jnp.where(first_core, far, own))
            tile = jnp.concatenate(pair, axis=0)
            m_ref[pl.ds(start, 2 * blk), lanes] = tile
            if r == 0:
                o_ref[:, lanes] = tile
    m = m_ref[...]
    s = dot(o_ref[...], m)
    kept = []
    for p in range(2):
        keep = keep_ref[2 + k, pl.ds(2 * row_id + p, 1)]
        kept.append(jnp.where(keep > 0, s[p * blk : (p + 1) * blk], 0.0).astype(jnp.bfloat16))
    res = purify(jnp.concatenate(kept, axis=0), m)
    mine = res[:, : 2 * blk]
    for j in range(1, line):
        mine = jnp.where(col_id // 2 == j, res[:, 2 * j * blk : (2 * j + 2) * blk], mine)
    first, second = split_pair(mine[:blk], mine[blk:])
    return jnp.where(first_core, first, second).astype(jnp.bfloat16)


def unpack_kernel(plan, kept_hbm, shift_hbm, ret_ref, *refs):
    *more_refs, out_hbm, rows_ref, shift_ref, stage, out_ref, m_ref, o_ref, sems = refs
    row_id, col_id = lax.axis_index("row"), lax.axis_index("col")
    blk = plan.blk
    chip = row_id * plan.line + col_id // 2
    copies = [
        pltpu.make_async_copy(shift_hbm, shift_ref, sems.at[0]),
        pltpu.make_async_copy(kept_hbm.at[pl.ds(2 * row_id, 2)], rows_ref, sems.at[1]),
    ]
    for copy in copies:
        copy.start()
    stage[: plan.ndev] = ret_ref[...]
    if plan.shared:
        half = plan.shared // 2
        for k in range(half):
            for i in range(2):
                stage[plan.ndev + 2 * k + i] = more_refs[0][i * half + k]
    for k in range(plan.extra):
        stage[plan.ndev + plan.shared + k] = extra_block(plan, k, *more_refs[1:], m_ref, o_ref)
    for copy in copies:
        copy.wait()
    part = rows_ref.shape[2] // 4
    copies = []
    for p in range(2):
        base = PANEL - 1 - shift_ref[2 * row_id + p]
        lanes = slice(p * blk, (p + 1) * blk)
        for e in range(rows_ref.shape[2]):
            tile = stage[plan.back_slot(rows_ref[p, col_id, e] + base, chip)]
            out_ref[p, :, e * blk : (e + 1) * blk] = tile[:, lanes].astype(jnp.float32)
            if e % part == part - 1:
                at = (p, slice(None), pl.ds((e + 1 - part) * blk, part * blk))
                copies.append(pltpu.make_async_copy(out_ref.at[at], out_hbm.at[at], sems.at[2 + len(copies)]))
                copies[-1].start()
    for copy in copies:
        copy.wait()


def swapped(shard, axis, by):
    return lax.ppermute(shard, axis, [(i, i ^ by) for i in range(lax.axis_size(axis))])


def body(density, density_rows, square_rows, panel_shift):
    both = ("row", "col")
    n_row, n_col = lax.axis_size("row"), lax.axis_size("col")
    blk, rh = density.shape[1], density_rows.shape[2]
    npan = density_rows.shape[0]
    plan = Plan(n_row, n_col, blk)
    ndev = plan.ndev
    bf16 = jnp.bfloat16
    size = n_col * blk
    square = pltpu.VMEM((size, size), bf16)
    tables = [pltpu.SMEM((2, npan, rh), jnp.int32), pltpu.SMEM((npan,), jnp.int32)]

    def blocks(*shape):
        return jax.ShapeDtypeStruct((*shape, 2 * blk), bf16)

    shapes = [blocks(ndev, blk)] + ([blocks(plan.slots, blk)] * plan.line if plan.shared else [])
    packed, *line = pl.pallas_call(
        functools.partial(pack_kernel, plan),
        out_shape=shapes,
        in_specs=[HBM] * 3,
        out_specs=[HBM] * len(shapes),
        scratch_shapes=[pltpu.VMEM(density.shape, bf16)]
        + tables
        + [
            pltpu.VMEM((ndev + plan.line * plan.slots, blk, 2 * blk), bf16),
            pltpu.SemaphoreType.DMA((max(4, len(shapes)),)),
        ],
        compiler_params=PACK_PARAMS,
        name="pack",
    )(density, density_rows, panel_shift)
    y = lax.all_to_all(packed, both, 0, 0, tiled=True)
    sets = 1 + (1 if plan.shared else 0) + plan.extra
    keep = pl.pallas_call(
        functools.partial(mask_kernel, plan),
        out_shape=jax.ShapeDtypeStruct((sets, npan, size), jnp.float32),
        in_specs=[SMEM, VMEM],
        out_specs=VMEM,
        compiler_params=PARAMS,
        name="masks",
    )(panel_shift, square_rows)
    back, extra = [], []
    if plan.shared:

        def regroup(kernel, shapes, name, *operands):
            return pl.pallas_call(
                functools.partial(kernel, plan),
                out_shape=shapes,
                in_specs=[VMEM] * len(operands),
                out_specs=[VMEM] * len(shapes),
                compiler_params=PARAMS,
                cost_estimate=pl.CostEstimate(flops=HINT, bytes_accessed=0, transcendentals=0),
                name=name,
            )(*operands)

        line = line[:1] + [swapped(sent, "col", 2 * i) for i, sent in enumerate(line) if i]
        shapes = [blocks(plan.line, blk)] * n_row + [blocks(plan.line * plan.extra, blk)] * min(1, plan.extra)
        plane = list(regroup(regroup_kernel, shapes, "regroup", *line))
        plane, rest = plane[:n_row], plane[n_row:]
        own = jnp.concatenate([plane[0]] + [swapped(sent, "row", r) for r, sent in enumerate(plane) if r])
        far = swapped(own, "col", 1)
        back = pl.pallas_call(
            functools.partial(shared_kernel, plan),
            out_shape=[blocks(plan.shared // 2, blk)] * 2,
            in_specs=[VMEM] * 3,
            out_specs=[VMEM] * 2,
            scratch_shapes=[square] * 2 + [pltpu.VMEM((plan.shared, blk, 2 * blk), bf16)],
            compiler_params=PARAMS,
            name="shared",
        )(keep, own, far)
        y, keep, first, *rest = lax.optimization_barrier((y, keep, back[0], *rest))
        back = [first, swapped(back[1], "col", plan.line)]
        shapes = [blocks(plan.line, blk)] * n_row + [blocks(plan.line * plan.extra, blk)] * min(1, plan.extra)
        back = list(regroup(return_kernel, shapes, "regroup_back", *back, *rest))
        back, rest = back[:n_row], back[n_row:]
        rest = rest + [swapped(sent, "row", r) for sent in rest for r in range(1, n_row)]
        back = [back[0]] + [swapped(sent, "row", r) for r, sent in enumerate(back) if r]
        back = pl.pallas_call(
            functools.partial(sort_kernel, plan),
            out_shape=[blocks(plan.shared // 2, blk)] * 2,
            in_specs=[VMEM] * n_row,
            out_specs=[VMEM] * 2,
            compiler_params=PARAMS,
            cost_estimate=pl.CostEstimate(flops=500_000_000, bytes_accessed=0, transcendentals=0),
            name="sort",
        )(*back)
        back = [back[0], swapped(back[1], "col", 2)]

        def join(hint, name, *parts):
            return pl.pallas_call(
                functools.partial(join_kernel, plan),
                out_shape=blocks(sum(part.shape[0] for part in parts), blk),
                in_specs=[VMEM] * len(parts),
                out_specs=VMEM,
                compiler_params=PARAMS,
                cost_estimate=pl.CostEstimate(flops=hint, bytes_accessed=0, transcendentals=0),
                name=name,
            )(*parts)

        back = [join(4_000_000_000, "join_back", *back)]
    if plan.extra:
        far = swapped(join(1_500_000_000, "join", *rest), "col", 1)
        far, *back = lax.optimization_barrier((far, *back))
        extra = [keep, far, *rest]
    out = pl.pallas_call(
        functools.partial(full_kernel, plan),
        out_shape=blocks(ndev, blk),
        in_specs=[VMEM] * 2,
        out_specs=VMEM,
        scratch_shapes=[square] * 2,
        compiler_params=PARAMS,
        cost_estimate=pl.CostEstimate(flops=4 * size**3, bytes_accessed=8 * ndev * blk * blk, transcendentals=0),
        name="full",
    )(keep, y)
    ret = lax.all_to_all(out, both, 0, 0, tiled=True)
    return pl.pallas_call(
        functools.partial(unpack_kernel, plan),
        out_shape=jax.ShapeDtypeStruct(density.shape, jnp.float32),
        in_specs=[HBM] * 2 + [VMEM] * (1 + len(back) + len(extra)),
        out_specs=HBM,
        scratch_shapes=tables
        + [
            pltpu.VMEM((ndev + plan.shared + plan.extra, blk, 2 * blk), bf16),
            pltpu.VMEM(density.shape, jnp.float32),
            square,
            pltpu.VMEM((2 * blk, size), bf16),
            pltpu.SemaphoreType.DMA((10,)),
        ],
        compiler_params=PARAMS,
        name="unpack",
    )(square_rows, panel_shift, ret, *back, *extra)


def solution(mesh):
    placed = (P("row", None, "col"), P(), P(), P())
    return jax.shard_map(
        body, mesh=mesh, in_specs=placed, out_specs=P("row", None, "col"), check_vma=False
    )
```

```python
import functools

import jax
import jax.numpy as jnp
from jax import lax
from jax.experimental import pallas as pl
from jax.experimental.pallas import tpu as pltpu
from jax.sharding import PartitionSpec as P

PANEL = 49

SMEM = pl.BlockSpec(memory_space=pltpu.SMEM)
VMEM = pl.BlockSpec(memory_space=pltpu.VMEM)
HBM = pl.BlockSpec(memory_space=pltpu.HBM)
PARAMS = pltpu.CompilerParams(vmem_limit_bytes=40 * 1024 * 1024)
HINT = 20_000_000_000
PACK_PARAMS = pltpu.CompilerParams(vmem_limit_bytes=63 * 1024 * 1024)


class Plan:
    def __init__(self, n_row, n_col, blk):
        self.n_row, self.n_col, self.blk = n_row, n_col, blk
        self.ndev = n_row * n_col
        self.line = n_col // 2
        chips = self.ndev // 2
        self.full = min(self.ndev, PANEL)
        self.shared = min(chips, PANEL - self.full)
        self.extra = PANEL - self.full - self.shared
        self.slots = self.n_row + self.extra if self.shared else 0

    def residue(self, at):
        return jnp.where(at < PANEL - 1, at + 1, at + 1 - PANEL)

    def send_slot(self, at, chip):
        u = self.residue(at)
        if not self.shared:
            return u
        apart = jnp.bitwise_xor(u - self.full, chip)
        shift = self.line.bit_length() - 1
        plane, line = jnp.right_shift(apart, shift), jnp.bitwise_and(apart, self.line - 1)
        beyond = u - self.full - self.shared
        slot = jnp.where(beyond < 0, line * self.slots + plane, self.n_row + beyond)
        return jnp.where(u < self.full, u, self.ndev + slot)

    def back_slot(self, at, chip):
        u = self.residue(at)
        if not self.shared:
            return u
        apart = jnp.bitwise_xor(u - self.full, chip)
        return self.ndev - self.full + jnp.where(
            jnp.logical_and(u >= self.full, u < self.full + self.shared), self.full + apart, u
        )


def kept_lanes(rows, u, shift, blk):
    npan = rows.shape[0]
    target = u + shift
    target = jnp.where(target >= PANEL, target - PANEL, target)
    has = jnp.sum((rows == target).astype(jnp.float32), axis=1, keepdims=True)
    lane = lax.broadcasted_iota(jnp.int32, (npan, npan * blk), 1)
    tile = lax.broadcasted_iota(jnp.int32, (npan, npan * blk), 0)
    return jnp.sum(jnp.where(lane // blk == tile, has, 0.0), axis=0, keepdims=True)


def pack_kernel(plan, x_hbm, rows_hbm, shift_hbm, *refs):
    *out_refs, x_ref, rows_ref, shift_ref, stage, sems = refs
    row_id, col_id = lax.axis_index("row"), lax.axis_index("col")
    blk, ndev, slots = plan.blk, plan.ndev, plan.slots
    chip = row_id * plan.line + col_id // 2
    copies = [
        pltpu.make_async_copy(shift_hbm, shift_ref, sems.at[0]),
        pltpu.make_async_copy(rows_hbm.at[pl.ds(2 * row_id, 2)], rows_ref, sems.at[1]),
        pltpu.make_async_copy(x_hbm.at[0], x_ref.at[0], sems.at[2]),
        pltpu.make_async_copy(x_hbm.at[1], x_ref.at[1], sems.at[3]),
    ]
    for copy in copies:
        copy.start()
    stage[...] = jnp.zeros_like(stage)
    for copy in copies[:2]:
        copy.wait()
    for p in range(2):
        copies[2 + p].wait()
        base = PANEL - 1 - shift_ref[2 * row_id + p]
        lanes = slice(p * blk, (p + 1) * blk)
        for e in range(rows_ref.shape[2]):
            slot = plan.send_slot(rows_ref[p, col_id, e] + base, chip)
            stage[slot, :, lanes] = x_ref[p, :, e * blk : (e + 1) * blk]
    for k in range(plan.extra):
        block = stage[ndev + plan.n_row + k]
        for i in range(1, plan.line):
            stage[ndev + i * slots + plan.n_row + k] = block
    spans = [(0, ndev)] + [(ndev + i * slots, slots) for i in range(len(out_refs) - 1)]
    copies = [
        pltpu.make_async_copy(stage.at[pl.ds(first, size)], ref, sems.at[i])
        for i, ((first, size), ref) in enumerate(zip(spans, out_refs))
    ]
    for copy in copies:
        copy.start()
    for copy in copies:
        copy.wait()


def mask_kernel(plan, shift_ref, kept_ref, keep_ref):
    me = lax.axis_index("row") * plan.n_col + lax.axis_index("col")
    sets = [jnp.minimum(me, plan.full - 1), plan.full + me // 2]
    sets += [plan.full + plan.shared + k for k in range(plan.extra)]
    for k, u in enumerate(sets[: keep_ref.shape[0]]):
        for panel in range(2 * plan.n_row):
            keep_ref[k, panel : panel + 1] = kept_lanes(kept_ref[panel], u, shift_ref[panel], plan.blk)


def split_pair(low, high):
    blk = low.shape[1] // 2
    first = jnp.concatenate([low[:, :blk], high[:, :blk]], axis=1)
    second = jnp.concatenate([low[:, blk:], high[:, blk:]], axis=1)
    return first, second


def dot(a, b):
    return jnp.dot(a, b, preferred_element_type=jnp.float32)


def purify(s, m):
    return 3.0 * s.astype(jnp.float32) - 2.0 * dot(s, m)


def mask_square(plan, s, keep_ref, k, s_ref):
    for panel in range(2 * plan.n_row):
        at = slice(panel * plan.blk, (panel + 1) * plan.blk)
        s_ref[at] = jnp.where(keep_ref[k, panel : panel + 1] > 0, s[at], 0.0).astype(jnp.bfloat16)


def full_kernel(plan, keep_ref, y_ref, res_ref, m_ref, s_ref):
    blk, n_col = plan.blk, plan.n_col
    for r in range(plan.n_row):
        for j in range(n_col // 2):
            src = r * n_col + 2 * j
            first, second = split_pair(y_ref[src], y_ref[src + 1])
            lanes = slice(2 * j * blk, (2 * j + 2) * blk)
            m_ref[2 * r * blk : (2 * r + 1) * blk, lanes] = first
            m_ref[(2 * r + 1) * blk : (2 * r + 2) * blk, lanes] = second
    m = m_ref[...]
    mask_square(plan, dot(m, m), keep_ref, 0, s_ref)
    for r in range(plan.n_row):
        res = purify(s_ref[2 * r * blk : (2 * r + 2) * blk], m).astype(jnp.bfloat16)
        for j in range(n_col // 2):
            lanes = slice(2 * j * blk, (2 * j + 2) * blk)
            to = r * n_col + 2 * j
            res_ref[to], res_ref[to + 1] = split_pair(res[:blk, lanes], res[blk:, lanes])


def regroup_kernel(plan, *refs):
    line, plane, extra = refs[: plan.line], refs[plan.line : plan.line + plan.n_row], refs[plan.line + plan.n_row :]
    for i, sent in enumerate(line):
        for r, ref in enumerate(plane):
            ref[i] = sent[r]
        for ref in extra:
            for k in range(plan.extra):
                ref[k * plan.line + i] = sent[plan.n_row + k]


def return_kernel(plan, *refs):
    passed = (len(refs) - 2 - plan.n_row) // 2
    ins, outs = refs[: 2 + passed], refs[2 + passed :]
    half = plan.line // 2
    for r in range(plan.n_row):
        for s in range(2):
            for i in range(half):
                outs[r][s * half + i] = ins[s][i * plan.n_row + r]
    for ref, to in zip(ins[2:], outs[plan.n_row :]):
        to[...] = ref[...]


def join_kernel(plan, *refs):
    *parts, out_ref = refs
    first = 0
    for ref in parts:
        out_ref[first : first + ref.shape[0]] = ref[...]
        first += ref.shape[0]


def sort_kernel(plan, *refs):
    plane, outs = refs[: plan.n_row], refs[plan.n_row :]
    for r, sent in enumerate(plane):
        for s in range(2):
            for i, ref in enumerate(outs):
                ref[2 * r + s] = sent[2 * s + i]


def shared_kernel(plan, keep_ref, own_ref, far_ref, *refs):
    *out_refs, m_ref, s_ref, res_ref = refs
    n_row, n_col, blk = plan.n_row, plan.n_col, plan.blk
    row_id, col_id = lax.axis_index("row"), lax.axis_index("col")
    first_core = col_id % 2 == 0
    for r in range(n_row):
        start = pl.multiple_of(jnp.bitwise_xor(row_id, r) * 2 * blk, 2 * blk)
        for j in range(plan.line):
            lanes = slice(2 * j * blk, (2 * j + 2) * blk)
            at = r * plan.line + jnp.bitwise_xor(col_id // 2, j)
            own, far = own_ref[at], far_ref[at]
            pair = split_pair(jnp.where(first_core, own, far), jnp.where(first_core, far, own))
            m_ref[pl.ds(start, 2 * blk), lanes] = jnp.concatenate(pair, axis=0)
    m = m_ref[...]
    mask_square(plan, dot(m, m), keep_ref, 1, s_ref)
    res = purify(s_ref[...], m).astype(jnp.bfloat16)
    for row in range(n_row):
        upper, lower = res[2 * row * blk : (2 * row + 1) * blk], res[(2 * row + 1) * blk : (2 * row + 2) * blk]
        for j in range(plan.line):
            lanes = slice(2 * j * blk, (2 * j + 2) * blk)
            first, second = split_pair(upper[:, lanes], lower[:, lanes])
            to = jnp.bitwise_xor(col_id // 2, j) * n_row + jnp.bitwise_xor(row_id, row)
            res_ref[to] = jnp.where(first_core, first, second)
    for i, ref in enumerate(out_refs):
        ref[...] = res_ref[i * ref.shape[0] : (i + 1) * ref.shape[0]]


def extra_block(plan, k, keep_ref, far_ref, *refs):
    own_refs, (m_ref, o_ref) = refs[: plan.n_row], refs[plan.n_row :]
    row_id, col_id = lax.axis_index("row"), lax.axis_index("col")
    first_core = col_id % 2 == 0
    blk, line = plan.blk, plan.line
    for r, own_ref in enumerate(own_refs):
        start = pl.multiple_of(jnp.bitwise_xor(row_id, r) * 2 * blk, 2 * blk)
        for j in range(line):
            lanes = slice(2 * j * blk, (2 * j + 2) * blk)
            at = k * line + jnp.bitwise_xor(col_id // 2, j)
            own, far = own_ref[at], far_ref[r * plan.extra * line + at]
            pair = split_pair(jnp.where(first_core, own, far), jnp.where(first_core, far, own))
            tile = jnp.concatenate(pair, axis=0)
            m_ref[pl.ds(start, 2 * blk), lanes] = tile
            if r == 0:
                o_ref[:, lanes] = tile
    m = m_ref[...]
    s = dot(o_ref[...], m)
    kept = []
    for p in range(2):
        keep = keep_ref[2 + k, pl.ds(2 * row_id + p, 1)]
        kept.append(jnp.where(keep > 0, s[p * blk : (p + 1) * blk], 0.0).astype(jnp.bfloat16))
    res = purify(jnp.concatenate(kept, axis=0), m)
    mine = res[:, : 2 * blk]
    for j in range(1, line):
        mine = jnp.where(col_id // 2 == j, res[:, 2 * j * blk : (2 * j + 2) * blk], mine)
    first, second = split_pair(mine[:blk], mine[blk:])
    return jnp.where(first_core, first, second).astype(jnp.bfloat16)


def unpack_kernel(plan, kept_hbm, shift_hbm, ret_ref, *refs):
    *more_refs, out_hbm, rows_ref, shift_ref, stage, out_ref, m_ref, o_ref, sems = refs
    row_id, col_id = lax.axis_index("row"), lax.axis_index("col")
    blk = plan.blk
    chip = row_id * plan.line + col_id // 2
    copies = [
        pltpu.make_async_copy(shift_hbm, shift_ref, sems.at[0]),
        pltpu.make_async_copy(kept_hbm.at[pl.ds(2 * row_id, 2)], rows_ref, sems.at[1]),
    ]
    for copy in copies:
        copy.start()
    stage[: plan.ndev] = ret_ref[...]
    if plan.shared:
        half = plan.shared // 2
        for k in range(half):
            for i in range(2):
                stage[plan.ndev + 2 * k + i] = more_refs[0][i * half + k]
    for k in range(plan.extra):
        stage[plan.ndev + plan.shared + k] = extra_block(plan, k, *more_refs[1:], m_ref, o_ref)
    for copy in copies:
        copy.wait()
    part = rows_ref.shape[2] // 4
    copies = []
    for p in range(2):
        base = PANEL - 1 - shift_ref[2 * row_id + p]
        lanes = slice(p * blk, (p + 1) * blk)
        for e in range(rows_ref.shape[2]):
            tile = stage[plan.back_slot(rows_ref[p, col_id, e] + base, chip)]
            out_ref[p, :, e * blk : (e + 1) * blk] = tile[:, lanes].astype(jnp.float32)
            if e % part == part - 1:
                at = (p, slice(None), pl.ds((e + 1 - part) * blk, part * blk))
                copies.append(pltpu.make_async_copy(out_ref.at[at], out_hbm.at[at], sems.at[2 + len(copies)]))
                copies[-1].start()
    for copy in copies:
        copy.wait()


def swapped(shard, axis, by):
    n_col = lax.axis_size("col")
    total = lax.axis_size("row") * n_col
    apart = by * (n_col if axis == "row" else 1)
    return lax.ppermute(shard, ("row", "col"), [(i, i ^ apart) for i in reversed(range(total))])


def body(density, density_rows, square_rows, panel_shift):
    both = ("row", "col")
    n_row, n_col = lax.axis_size("row"), lax.axis_size("col")
    blk, rh = density.shape[1], density_rows.shape[2]
    npan = density_rows.shape[0]
    plan = Plan(n_row, n_col, blk)
    ndev = plan.ndev
    bf16 = jnp.bfloat16
    size = n_col * blk
    square = pltpu.VMEM((size, size), bf16)
    tables = [pltpu.SMEM((2, npan, rh), jnp.int32), pltpu.SMEM((npan,), jnp.int32)]

    def blocks(*shape):
        return jax.ShapeDtypeStruct((*shape, 2 * blk), bf16)

    shapes = [blocks(ndev, blk)] + ([blocks(plan.slots, blk)] * plan.line if plan.shared else [])
    packed, *line = pl.pallas_call(
        functools.partial(pack_kernel, plan),
        out_shape=shapes,
        in_specs=[HBM] * 3,
        out_specs=[HBM] * len(shapes),
        scratch_shapes=[pltpu.VMEM(density.shape, bf16)]
        + tables
        + [
            pltpu.VMEM((ndev + plan.line * plan.slots, blk, 2 * blk), bf16),
            pltpu.SemaphoreType.DMA((max(4, len(shapes)),)),
        ],
        compiler_params=PACK_PARAMS,
        name="pack",
    )(density, density_rows, panel_shift)
    y = lax.all_to_all(packed, both, 0, 0, tiled=True)
    sets = 1 + (1 if plan.shared else 0) + plan.extra
    keep = pl.pallas_call(
        functools.partial(mask_kernel, plan),
        out_shape=jax.ShapeDtypeStruct((sets, npan, size), jnp.float32),
        in_specs=[SMEM, VMEM],
        out_specs=VMEM,
        compiler_params=PARAMS,
        name="masks",
    )(panel_shift, square_rows)
    back, extra = [], []
    if plan.shared:

        def regroup(kernel, shapes, name, *operands):
            return pl.pallas_call(
                functools.partial(kernel, plan),
                out_shape=shapes,
                in_specs=[VMEM] * len(operands),
                out_specs=[VMEM] * len(shapes),
                compiler_params=PARAMS,
                cost_estimate=pl.CostEstimate(flops=HINT, bytes_accessed=0, transcendentals=0),
                name=name,
            )(*operands)

        line = line[:1] + [swapped(sent, "col", 2 * i) for i, sent in enumerate(line) if i]
        shapes = [blocks(plan.line, blk)] * n_row + [blocks(plan.line * plan.extra, blk)] * min(1, plan.extra)
        plane = list(regroup(regroup_kernel, shapes, "regroup", *line))
        plane, rest = plane[:n_row], plane[n_row:]
        own = jnp.concatenate([plane[0]] + [swapped(sent, "row", r) for r, sent in enumerate(plane) if r])
        far = swapped(own, "col", 1)
        back = pl.pallas_call(
            functools.partial(shared_kernel, plan),
            out_shape=[blocks(plan.shared // 2, blk)] * 2,
            in_specs=[VMEM] * 3,
            out_specs=[VMEM] * 2,
            scratch_shapes=[square] * 2 + [pltpu.VMEM((plan.shared, blk, 2 * blk), bf16)],
            compiler_params=PARAMS,
            name="shared",
        )(keep, own, far)
        y, keep, first, *rest = lax.optimization_barrier((y, keep, back[0], *rest))
        back = [first, swapped(back[1], "col", plan.line)]
        shapes = [blocks(plan.line, blk)] * n_row + [blocks(plan.line * plan.extra, blk)] * min(1, plan.extra)
        back = list(regroup(return_kernel, shapes, "regroup_back", *back, *rest))
        back, rest = back[:n_row], back[n_row:]
        rest = rest + [swapped(sent, "row", r) for sent in rest for r in range(1, n_row)]
        back = [back[0]] + [swapped(sent, "row", r) for r, sent in enumerate(back) if r]
        back = pl.pallas_call(
            functools.partial(sort_kernel, plan),
            out_shape=[blocks(plan.shared // 2, blk)] * 2,
            in_specs=[VMEM] * n_row,
            out_specs=[VMEM] * 2,
            compiler_params=PARAMS,
            cost_estimate=pl.CostEstimate(flops=500_000_000, bytes_accessed=0, transcendentals=0),
            name="sort",
        )(*back)
        back = [back[0], swapped(back[1], "col", 2)]

        def join(hint, name, *parts):
            return pl.pallas_call(
                functools.partial(join_kernel, plan),
                out_shape=blocks(sum(part.shape[0] for part in parts), blk),
                in_specs=[VMEM] * len(parts),
                out_specs=VMEM,
                compiler_params=PARAMS,
                cost_estimate=pl.CostEstimate(flops=hint, bytes_accessed=0, transcendentals=0),
                name=name,
            )(*parts)

        back = [join(4_000_000_000, "join_back", *back)]
    if plan.extra:
        far = swapped(join(1_500_000_000, "join", *rest), "col", 1)
        far, *back = lax.optimization_barrier((far, *back))
        extra = [keep, far, *rest]
    out = pl.pallas_call(
        functools.partial(full_kernel, plan),
        out_shape=blocks(ndev, blk),
        in_specs=[VMEM] * 2,
        out_specs=VMEM,
        scratch_shapes=[square] * 2,
        compiler_params=PARAMS,
        cost_estimate=pl.CostEstimate(flops=4 * size**3, bytes_accessed=8 * ndev * blk * blk, transcendentals=0),
        name="full",
    )(keep, y)
    ret = lax.all_to_all(out, both, 0, 0, tiled=True)
    return pl.pallas_call(
        functools.partial(unpack_kernel, plan),
        out_shape=jax.ShapeDtypeStruct(density.shape, jnp.float32),
        in_specs=[HBM] * 2 + [VMEM] * (1 + len(back) + len(extra)),
        out_specs=HBM,
        scratch_shapes=tables
        + [
            pltpu.VMEM((ndev + plan.shared + plan.extra, blk, 2 * blk), bf16),
            pltpu.VMEM(density.shape, jnp.float32),
            square,
            pltpu.VMEM((2 * blk, size), bf16),
            pltpu.SemaphoreType.DMA((10,)),
        ],
        compiler_params=PARAMS,
        name="unpack",
    )(square_rows, panel_shift, ret, *back, *extra)


def solution(mesh):
    placed = (P("row", None, "col"), P(), P(), P())
    return jax.shard_map(
        body, mesh=mesh, in_specs=placed, out_specs=P("row", None, "col"), check_vma=False
    )
```
